32 devices in a mesh: gx: 8 (over z, y), gy: 4 (over x, core).
Axes of the slice: x: 2, y: 2, z: 4, core: 2. Of those that a mesh axis runs over, the one named last changes fastest.
Arguments:
- temper_start: float32 [256, 256, 256], P('gx', 'gy'), may hold values from -4 to 4
- cure_start: float32 [256, 256, 256], P('gx', 'gy'), may hold values from 0.05 to 0.9
- temper_middle: float32 [256, 256, 256], P('gx', 'gy'), may hold values from -4 to 4
- cure_middle: float32 [256, 256, 256], P('gx', 'gy'), may hold values from 0.05 to 0.9
- adjoint_temper: float32 [256, 256, 256], P('gx', 'gy'), may hold values from -6 to 6
- adjoint_cure: float32 [256, 256, 256], P('gx', 'gy'), may hold values from -6 to 6
- conduct_first: float32 [264], P('gx'), may hold values from 0 to 3000, as said below
- inverse_first: float32 [256, 32], P('gx'), may hold values from 0 to 1, as said below
- conduct_second: float32 [260], P('gy'), may hold values from 0 to 3000, as said below
- inverse_second: float32 [256, 64], P('gy'), may hold values from 0 to 1, as said below
- conduct_thick: float32 [257], replicated, may hold values from 20 to 120
- inverse_thick: float32 [256, 256], replicated, may hold values from 0 to 1, as said below
Outputs:
- sensitivity_temper: float32 [256, 256, 256], P('gx', 'gy')
- sensitivity_cure: float32 [256, 256, 256], P('gx', 'gy')
The draws below stay inside these ranges and needn't reach their ends.
Inputs may be any that keep to these rules, and one draw needn't show every extreme that they name: `conduct_first`: group j of 33 entries holds the left faces of its 32 cells and then the face beyond them; entry 32 of group j equals entry 0 of group j + 1, and the last group's entry 32 is 0 (insulated side). `inverse_first`: rows j * 32 to (j + 1) * 32 - 1 are the inverse of group j's diagonal block of I + Kx restricted to that group: diagonal 1 plus the cell's two faces, off-diagonals minus the faces between its cells. `conduct_second`: group j of 65 entries holds the left faces of its 64 cells and then the face beyond them; entry 64 of group j equals entry 0 of group j + 1, and the last group's entry 64 is 0 (insulated side). `inverse_second`: rows j * 64 to (j + 1) * 64 - 1 are the inverse of group j's diagonal block of I + Ky restricted to that group. `inverse_thick`: the inverse of I + Kz through the thickness.
All inputs are finite; a program needn't handle non-finite values.
Results may differ from the reference program's by a relative error of at most 0.0003.
Values sent between devices are 32-bit elements; how exact they have to be, the bound alone decides.
A program may use at most 128 MiB of HBM per device.

```python
import jax
import jax.numpy as jnp
from jax import lax

CX = 32
CY = 64
NZ = 256
NX = 256
NY = 256


def group_system(key, groups, width, insulated, shown_low, shown_high):
    total = groups * width
    logs = jax.random.uniform(key, (total + 1,), jnp.float32, jnp.log(shown_low), jnp.log(shown_high))
    raw = jnp.exp(logs)
    if insulated:
        raw = jnp.where(jnp.arange(total + 1) == total, 0.0, raw)
    positions = jnp.arange(groups)[:, None] * width + jnp.arange(width + 1)[None, :]
    faces = raw[positions]
    diagonal = 1.0 + faces[:, :-1] + faces[:, 1:]
    inner = -faces[:, 1:-1]
    zero_column = jnp.zeros((groups, 1), jnp.float32)
    below = jnp.concatenate([zero_column, inner], axis=1)
    above = jnp.concatenate([inner, zero_column], axis=1)
    identity = jnp.broadcast_to(jnp.eye(width, dtype=jnp.float32), (groups, width, width))
    inverse = lax.linalg.tridiagonal_solve(below, diagonal, above, identity)
    return (faces.reshape(-1), inverse.reshape(total, width))


def draw_conduct_first(key, part):
    return group_system(jax.random.fold_in(key, 101), NX // CX, CX, True, 400.0, 2500.0)[0]


def draw_inverse_first(key, part):
    return group_system(jax.random.fold_in(key, 101), NX // CX, CX, True, 400.0, 2500.0)[1]


def draw_conduct_second(key, part):
    return group_system(jax.random.fold_in(key, 202), NY // CY, CY, True, 400.0, 2500.0)[0]


def draw_inverse_second(key, part):
    return group_system(jax.random.fold_in(key, 202), NY // CY, CY, True, 400.0, 2500.0)[1]


def draw_conduct_thick(key, part):
    return group_system(jax.random.fold_in(key, 303), 1, NZ, False, 30.0, 80.0)[0]


def draw_inverse_thick(key, part):
    return group_system(jax.random.fold_in(key, 303), 1, NZ, False, 30.0, 80.0)[1]


def level_of(stream_key, extent, pieces, least, largest):
    gain = 1.0
    for position, blocks in pieces:
        heights = jax.random.uniform(jax.random.fold_in(jax.random.fold_in(stream_key, 6), position), (blocks,), jnp.float32, least / len(pieces), largest / len(pieces))
        gain = gain * jnp.repeat(jnp.exp(heights), extent[position] // blocks).reshape((-1,) + (1,) * (len(extent) - 1 - position))
    return gain


def centred(key, extent, spread, reach, shards=(), kind=jnp.bfloat16):
    entries = spread * jax.random.normal(key, extent, jnp.float32)
    if shards:
        entries = entries * level_of(key, extent, shards, -0.22, 0.18)
    return jnp.clip(entries, -reach, reach).astype(kind)


def setup_inputs(seed: int = 0) -> dict:
    key_of = jax.random.split(jax.random.key(seed), 13)
    return {
        "temper_start": centred(key_of[0], (NX, NY, NZ), 0.8, 4.0, ((0, 8), (1, 4)), jnp.float32),
        "cure_start": jnp.clip(0.05 + 0.84999998 * jax.random.uniform(key_of[1], (NX, NY, NZ), jnp.float32) ** level_of(key_of[1], (NX, NY, NZ), ((0, 8), (1, 4)), -0.2, 0.2), 0.05, 0.9),
        "temper_middle": centred(key_of[2], (NX, NY, NZ), 0.8, 4.0, ((0, 8), (1, 4)), jnp.float32),
        "cure_middle": jnp.clip(0.05 + 0.84999998 * jax.random.uniform(key_of[3], (NX, NY, NZ), jnp.float32) ** level_of(key_of[3], (NX, NY, NZ), ((0, 8), (1, 4)), -0.2, 0.2), 0.05, 0.9),
        "adjoint_temper": centred(key_of[4], (NX, NY, NZ), 1.0, 6.0, ((0, 8), (1, 4)), jnp.float32),
        "adjoint_cure": centred(key_of[5], (NX, NY, NZ), 1.0, 6.0, ((0, 8), (1, 4)), jnp.float32),
        "conduct_first": draw_conduct_first(jax.random.fold_in(key_of[12], 71), 0),
        "inverse_first": draw_inverse_first(jax.random.fold_in(key_of[12], 71), 0),
        "conduct_second": draw_conduct_second(jax.random.fold_in(key_of[12], 71), 0),
        "inverse_second": draw_inverse_second(jax.random.fold_in(key_of[12], 71), 0),
        "conduct_thick": draw_conduct_thick(jax.random.fold_in(key_of[12], 71), 0),
        "inverse_thick": draw_inverse_thick(jax.random.fold_in(key_of[12], 71), 0),
    }


explicit_part = 2.0
heat_release = 100.0
cure_step = 0.5
arrhenius = 0.5
initial_rate = 0.1
highest = lax.Precision.HIGHEST

def reduced_solve(first_tip, last_tip, spike_ends):
    empty_row = jnp.zeros_like(first_tip[:1])

    def forward(running, inputs):
        corner_prev, partial_prev = running
        tail_here, head_next, left_here, right_here, value_last, value_first = inputs
        upper_entry = -tail_here - left_here * right_here * corner_prev
        lower_entry = -head_next
        determinant = 1.0 - upper_entry * lower_entry
        corner = -upper_entry / determinant
        bottom = 1.0 / determinant
        shifted = value_last + left_here * partial_prev
        solved_top = bottom * shifted + corner * value_first
        solved_low = -lower_entry / determinant * shifted + bottom * value_first
        return ((corner, solved_top), (solved_top, solved_low, corner, bottom))
    start_state = (jnp.zeros((), jnp.float32), jnp.zeros_like(first_tip[0]))
    inputs = (spike_ends[:-1, 3], spike_ends[1:, 0], spike_ends[:-1, 1], spike_ends[:-1, 2], last_tip[:-1], first_tip[1:])
    unused, (tops, lows, corners, bottoms) = lax.scan(forward, start_state, inputs)

    def backward(next_low, inputs):
        solved_top, solved_low, corner, bottom, right_next = inputs
        top_value = solved_top + corner * right_next * next_low
        low_value = solved_low + bottom * right_next * next_low
        return (low_value, (top_value, low_value))
    unused, (top_values, low_values) = lax.scan(backward, jnp.zeros_like(first_tip[0]), (tops, lows, corners, bottoms, spike_ends[1:, 2]), reverse=True)
    next_first = jnp.concatenate([low_values, empty_row], axis=0)
    prev_last = jnp.concatenate([empty_row, top_values], axis=0)
    return (next_first, prev_last)

def group_solve(right_side, inverse, faces, width):
    groups = right_side.shape[0] // width
    blocks = inverse.reshape(groups, width, width)
    blockwise = jnp.einsum('jba,jbl->jal', blocks, right_side.reshape(groups, width, -1), precision=highest)
    edges = faces.reshape(groups, width + 1)
    left_spike = edges[:, :1] * blocks[:, 0, :]
    right_spike = edges[:, width:] * blocks[:, width - 1, :]
    spike_ends = jnp.stack([left_spike[:, 0], left_spike[:, -1], right_spike[:, 0], right_spike[:, -1]], axis=1)
    next_first, prev_last = reduced_solve(blockwise[:, 0], blockwise[:, -1], spike_ends)
    result = blockwise + left_spike[:, :, None] * prev_last[:, None, :] + right_spike[:, :, None] * next_first[:, None, :]
    return result.reshape(groups * width, -1)

def along_axis(values, faces, width, axis):
    moved = jnp.moveaxis(values, axis, 0)
    length = moved.shape[0]
    edges = faces.reshape(-1, width + 1)
    left_face = edges[:, :width].reshape(length)[:, None, None]
    right_face = edges[:, 1:].reshape(length)[:, None, None]
    zero_layer = jnp.zeros_like(moved[:1])
    below = jnp.concatenate([zero_layer, moved[:-1]], axis=0)
    above = jnp.concatenate([moved[1:], zero_layer], axis=0)
    term = left_face * (moved - below) + right_face * (moved - above)
    return jnp.moveaxis(term, 0, axis)

def stiffness(field, conduct_first, conduct_second, conduct_thick):
    total = along_axis(field, conduct_first, CX, 0)
    total = total + along_axis(field, conduct_second, CY, 1)
    return total + along_axis(field, conduct_thick, NZ, 2)

def reference(temper_start, cure_start, temper_middle, cure_middle, adjoint_temper, adjoint_cure, conduct_first, inverse_first, conduct_second, inverse_second, conduct_thick, inverse_thick):
    temp_adjoint = adjoint_temper
    cure_adjoint = adjoint_cure
    for temper, cure in ((temper_middle, cure_middle), (temper_start, cure_start)):
        heating = jnp.exp(arrhenius * temper)
        remain = 1.0 - cure
        rate = heating * (initial_rate + cure) * remain * remain
        rate_temp = arrhenius * rate
        rate_cure = heating * (remain * remain - 2.0 * (initial_rate + cure) * remain)
        size_a, size_b, size_c = temp_adjoint.shape
        through = jnp.dot(temp_adjoint.reshape(-1, size_c), inverse_thick, precision=highest).reshape(size_a, size_b, size_c)
        moved = jnp.moveaxis(through, 1, 0).reshape(size_b, -1)
        second_done = group_solve(moved, inverse_second, conduct_second, CY).reshape(size_b, size_a, size_c)
        second_done = jnp.moveaxis(second_done, 0, 1)
        adjoint_flux = group_solve(second_done.reshape(size_a, -1), inverse_first, conduct_first, CX).reshape(size_a, size_b, size_c)
        source = heat_release * adjoint_flux + cure_step * cure_adjoint
        kick = stiffness(adjoint_flux, conduct_first, conduct_second, conduct_thick)
        temp_adjoint = temp_adjoint - explicit_part * kick + rate_temp * source
        cure_adjoint = cure_adjoint + rate_cure * source
    return (temp_adjoint, cure_adjoint)
```

```python
import functools

import jax
import jax.numpy as jnp
from jax import lax
from jax.experimental import pallas as pl
from jax.experimental.pallas import tpu as pltpu
from jax.sharding import PartitionSpec as P

explicit_part = 2.0
heat_release = 100.0
cure_step = 0.5
arrhenius = 0.5
initial_rate = 0.1
highest = lax.Precision.HIGHEST
MESH = pl.DeviceIdType.MESH
MARGIN = 8


def dot(a, b):
    return jnp.dot(a, b, precision=highest, preferred_element_type=jnp.float32)


def reduced_coefficients(ends, coef, count):
    corner = None
    for k in range(count - 1):
        upper = ends[k, 3:4]
        if corner is not None:
            upper = upper + ends[k, 1:2] * ends[k, 2:3] * corner
        head = ends[k + 1, 0:1]
        bottom = 1.0 / (1.0 - upper * head)
        corner = upper * bottom
        right_next = ends[k + 1, 2:3]
        coef[k, 0:1] = bottom
        coef[k, 1:2] = corner
        coef[k, 2:3] = head * bottom
        coef[k, 3:4] = ends[k, 1:2]
        coef[k, 4:5] = bottom * right_next
        coef[k, 5:6] = corner * right_next


def reduced_solve(first, last, coef, count):
    tops, lows = [], []
    for k in range(count - 1):
        shifted = last(k)
        if k:
            shifted = shifted + coef[k, 3:4] * tops[-1]
        follow = first(k + 1)
        tops.append(coef[k, 0:1] * shifted + coef[k, 1:2] * follow)
        lows.append(coef[k, 2:3] * shifted + coef[k, 0:1] * follow)
    for k in range(count - 3, -1, -1):
        tops[k] = tops[k] + coef[k, 5:6] * lows[k + 1]
        lows[k] = lows[k] + coef[k, 4:5] * lows[k + 1]
    zero = jnp.zeros_like(first(0))
    return lows + [zero], [zero] + tops


def kernel(
    nx,
    ny,
    ts_hbm,
    cs_hbm,
    tm_hbm,
    cm_hbm,
    al_hbm,
    ac_hbm,
    cf,
    bxs,
    bx,
    c2,
    by,
    ct,
    iz,
    out_t,
    out_c,
    lu,
    lc,
    t_mid,
    c_mid,
    t_start,
    c_start,
    g,
    mu,
    u,
    cya,
    cyb,
    wy0,
    wy1,
    ly,
    ry,
    tm_coef,
    tc_coef,
    zr,
    exs,
    exr,
    eys,
    eyr,
    coefx,
    coefy,
    xas,
    xar,
    xbs,
    xbr,
    yas,
    yar,
    ybs,
    ybr,
    eas,
    ear,
    eay,
    ebs,
    ebr,
    ebx,
    load_sem,
    store_sem,
    gx_send,
    gx_recv,
    gy_send,
    gy_recv,
):
    lx, lyn, nz = lu.shape
    rx = lyn // nx
    ryn = lx // ny
    mex = lax.axis_index("gx")
    mey = lax.axis_index("gy")
    sides = {"gx": (nx, mex, gx_send, gx_recv), "gy": (ny, mey, gy_send, gy_recv)}

    barrier = pltpu.get_barrier_semaphore()
    for axis, (count, me, _, _) in sides.items():
        for k in range(1, count):
            pl.semaphore_signal(
                barrier,
                inc=1,
                device_id={axis: lax.rem(me + k, count)},
                device_id_type=MESH,
            )

    loads = [
        pltpu.make_async_copy(source, target, load_sem.at[n])
        for n, (source, target) in enumerate(
            (
                (al_hbm, lu),
                (tm_hbm, t_mid),
                (cm_hbm, c_mid),
                (ac_hbm, lc),
                (ts_hbm, t_start),
                (cs_hbm, c_start),
            )
        )
    ]
    for load in loads:
        load.start()

    started = []

    def exchange(axis, kind, source, target):
        count, me, send, recv = sides[axis]
        copies = []
        for k in range(1, count):
            peer = lax.rem(me + k, count)
            copy = pltpu.make_async_remote_copy(
                src_ref=source(peer),
                dst_ref=target,
                send_sem=send.at[kind, k],
                recv_sem=recv.at[kind, k],
                device_id={axis: peer},
                device_id_type=MESH,
            )
            copy.start()
            copies.append(copy)
        started.extend(copies)
        return copies

    def arrive(copies):
        for copy in copies:
            copy.wait_recv()

    def row(value):
        return jnp.broadcast_to(value, (1, nz))

    a0, a1 = cf[0], cf[lx]
    exs[...] = jnp.zeros_like(exs)
    eys[...] = jnp.zeros_like(eys)
    exs[0:1] = row(a0 * bxs[0, 0])
    exs[1:2] = row(a0 * bxs[0, lx - 1])
    exs[2:3] = row(a1 * bxs[lx - 1, 0])
    exs[3:4] = row(a1 * bxs[lx - 1, lx - 1])
    s0, s1 = c2[0], c2[lyn]
    eys[0:1] = row(by[0:1, 0:1]) * s0
    eys[1:2] = row(by[0:1, lyn - 1 : lyn]) * s0
    eys[2:3] = row(by[lyn - 1 : lyn, 0:1]) * s1
    eys[3:4] = row(by[lyn - 1 : lyn, lyn - 1 : lyn]) * s1
    pl.semaphore_wait(barrier, nx + ny - 2)
    ends_x = exchange("gx", 0, lambda peer: exs, exr.at[mex])
    ends_y = exchange("gy", 0, lambda peer: eys, eyr.at[mey])
    exr[mex] = exs[...]
    eyr[mey] = eys[...]

    def second_faces(j, carry):
        cya[pl.ds(j, 1)] = row(c2[j])
        cyb[pl.ds(j, 1)] = row(c2[j + 1])
        return carry

    lax.fori_loop(0, lyn, second_faces, 0)
    wy0[...] = jnp.broadcast_to(by[:, 0:1], (lyn, nz))
    wy1[...] = jnp.broadcast_to(by[:, lyn - 1 : lyn], (lyn, nz))
    ly[...] = wy0[...] * s0
    ry[...] = wy1[...] * s1
    eas[...] = jnp.zeros_like(eas)
    ebs[...] = jnp.zeros_like(ebs)
    zr[...] = jnp.zeros_like(zr)

    def eliminate(i, keep):
        partial = 1.0 + cf[i] * keep
        scale = 1.0 / (partial + cf[i + 1])
        tm_coef[i] = scale
        tc_coef[i] = cf[i + 1] * scale
        return partial * scale

    lax.fori_loop(0, lx, eliminate, jnp.ones((1, nz), jnp.float32))

    face_low = ct[:, 0:nz]
    face_high = ct[:, 1 : nz + 1]

    for step in range(2):
        temper, cure = ((t_mid, c_mid), (t_start, c_start))[step]
        if step == 0:
            loads[0].wait()

        def tips(i, carry):
            first, last = carry
            slab = lu[i]
            u[pl.ds(i, 1), 0:nz] = jnp.sum(slab * wy0[...], axis=0, keepdims=True)
            u[pl.ds(i, 1), nz : 2 * nz] = jnp.sum(slab * wy1[...], axis=0, keepdims=True)
            return first + bxs[i, 0] * slab, last + bxs[i, lx - 1] * slab

        empty = jnp.zeros((lyn, nz), jnp.float32)
        first, last = lax.fori_loop(0, lx, tips, (empty, empty))
        tip_x = dot(by[...], jnp.concatenate([first, last], axis=1))
        for d in range(nx):
            xas[step, d, 0] = tip_x[d * rx : (d + 1) * rx, 0:nz]
            xas[step, d, 1] = tip_x[d * rx : (d + 1) * rx, nz:]
        out_xa = exchange("gx", 1 + 3 * step, lambda peer: xas.at[step, peer], xar.at[step, mex])
        eas[step, 0:1] = tip_x[0:1, 0:nz]
        eas[step, 1:2] = tip_x[0:1, nz:]
        eas[step, 2:3] = tip_x[lyn - 1 : lyn, 0:nz]
        eas[step, 3:4] = tip_x[lyn - 1 : lyn, nz:]
        out_ea = exchange("gy", 3 + 3 * step, lambda peer: eas.at[step], ear.at[step, mey])
        tip_y = dot(bx[...], u[...])
        for d in range(ny):
            yas[step, d, 0] = tip_y[d * ryn : (d + 1) * ryn, 0:nz]
            yas[step, d, 1] = tip_y[d * ryn : (d + 1) * ryn, nz:]
        out_ya = exchange("gy", 1 + 3 * step, lambda peer: yas.at[step, peer], yar.at[step, mey])
        xar[step, mex] = xas[step, mex]
        yar[step, mey] = yas[step, mey]
        ear[step, mey] = eas[step]

        def forward(i, before):
            value = (dot(by[...], lu[i]) + cf[i] * before) * tm_coef[i]
            g[i] = value
            return value

        lax.fori_loop(0, lx, forward, empty)

        if step == 0:
            arrive(ends_x)
            arrive(ends_y)
            reduced_coefficients(exr, coefx, nx)
            reduced_coefficients(eyr, coefy, ny)
        arrive(out_xa)
        lows, tops = reduced_solve(
            lambda k: xar[step, k, 0], lambda k: xar[step, k, 1], coefx, nx
        )
        for d in range(nx):
            xbs[step, d, 0] = lows[d]
            xbs[step, d, 1] = tops[d]
        out_xb = exchange("gx", 2 + 3 * step, lambda peer: xbs.at[step, peer], xbr.at[step, mex])
        arrive(out_ea)
        lows, tops = reduced_solve(
            lambda k: ear[step, k, 0:2], lambda k: ear[step, k, 2:4], coefy, ny
        )
        for d in range(ny):
            eay[d, 0:2] = lows[d]
            eay[d, 2:4] = tops[d]
        edge = eay[mey]
        ebs[step, 0:1] = edge[0:1]
        ebs[step, 1:2] = edge[2:3]
        ebs[step, 2:3] = edge[1:2]
        ebs[step, 3:4] = edge[3:4]
        out_eb = exchange("gx", 3 + 3 * step, lambda peer: ebs.at[step], ebr.at[step, mex])
        arrive(out_ya)
        lows, tops = reduced_solve(
            lambda k: yar[step, k, 0], lambda k: yar[step, k, 1], coefy, ny
        )
        for d in range(ny):
            ybs[step, d, 0] = lows[d]
            ybs[step, d, 1] = tops[d]
        out_yb = exchange("gy", 2 + 3 * step, lambda peer: ybs.at[step, peer], ybr.at[step, mey])
        xbr[step, mex] = xbs[step, mex]
        ybr[step, mey] = ybs[step, mey]
        ebr[step, mex] = ebs[step]

        def backward(n, after):
            i = lx - 1 - n
            value = g[i] + tc_coef[i] * after
            g[i] = value
            return value

        lax.fori_loop(0, lx, backward, empty)

        wide = 8

        def through(n, carry):
            block = g[pl.ds(n * wide, wide)].reshape(wide * lyn, nz)
            done = dot(block, iz[...]).reshape(wide, lyn, nz)
            mu[pl.ds(1 + n * wide, wide), MARGIN : MARGIN + lyn] = done
            return carry

        lax.fori_loop(0, lx // wide, through, 0)

        if step == 0:
            for n in (1, 2, 3):
                loads[n].wait()
        else:
            loads[4].wait()
            loads[5].wait()

        def rates(i, carry):
            heating = jnp.exp(arrhenius * temper[i])
            value = cure[i]
            remain = 1.0 - value
            grown = initial_rate + value
            temper[i] = arrhenius * (heating * grown * remain * remain)
            cure[i] = heating * (remain * remain - 2.0 * grown * remain)
            return carry

        lax.fori_loop(0, lx, rates, 0)

        arrive(out_eb)
        lows, tops = reduced_solve(
            lambda k: ebr[step, k, 0:2], lambda k: ebr[step, k, 2:4], coefx, nx
        )
        for d in range(nx):
            ebx[d, 0:2] = lows[d]
            ebx[d, 2:4] = tops[d]
        arrive(out_xb)
        arrive(out_yb)
        for d in range(nx):
            zr[d * rx : (d + 1) * rx] = xbr[step, d, 0]
            zr[lyn + d * rx : lyn + (d + 1) * rx] = xbr[step, d, 1]
        base = 2 * lyn
        for d in range(ny):
            zr[base + d * ryn : base + (d + 1) * ryn] = ybr[step, d, 0]
            zr[base + lx + d * ryn : base + lx + (d + 1) * ryn] = ybr[step, d, 1]
        corner = base + 2 * lx
        zr[corner : corner + 4] = ebx[mex, 0:4]
        zr[...] = dot(zr[...], iz[...])
        next_next = zr[corner : corner + 1]
        next_prev = zr[corner + 1 : corner + 2]
        prev_next = zr[corner + 2 : corner + 3]
        prev_prev = zr[corner + 3 : corner + 4]
        inside = slice(MARGIN, MARGIN + lyn)
        mu[lx + 1, inside] = zr[0:lyn] + ly[...] * next_prev + ry[...] * next_next
        mu[0, inside] = zr[lyn : 2 * lyn] + ly[...] * prev_prev + ry[...] * prev_next

        def correct(i, carry):
            left = a0 * bxs[0, i]
            right = a1 * bxs[lx - 1, i]
            y_next = zr[pl.ds(base + i, 1)]
            y_prev = zr[pl.ds(base + lx + i, 1)]
            mu[i + 1, inside] = (
                mu[i + 1, inside]
                + left * mu[0, inside]
                + right * mu[lx + 1, inside]
                + ly[...] * y_prev
                + ry[...] * y_next
            )
            mu[i + 1, MARGIN - 1 : MARGIN] = y_prev + left * prev_prev + right * next_prev
            mu[i + 1, MARGIN + lyn : MARGIN + lyn + 1] = (
                y_next + left * prev_next + right * next_next
            )
            return carry

        lax.fori_loop(0, lx, correct, 0)

        chunk = 16
        lane = lax.broadcasted_iota(jnp.int32, (chunk, nz), 1)

        def update(i, carry):
            for y in range(0, lyn, chunk):
                here = slice(y, y + chunk)
                start = MARGIN + y
                value = mu[i + 1, start : start + chunk]
                below = jnp.where(lane == 0, 0.0, pltpu.roll(value, 1, 1))
                above = jnp.where(lane == nz - 1, 0.0, pltpu.roll(value, nz - 1, 1))
                kick = (
                    cf[i] * (value - mu[i, start : start + chunk])
                    + cf[i + 1] * (value - mu[i + 2, start : start + chunk])
                    + cya[here] * (value - mu[i + 1, start - 1 : start + chunk - 1])
                    + cyb[here] * (value - mu[i + 1, start + 1 : start + chunk + 1])
                    + face_low * (value - below)
                    + face_high * (value - above)
                )
                old = lc[i, here]
                source = heat_release * value + cure_step * old
                lu[i, here] = lu[i, here] - explicit_part * kick + temper[i, here] * source
                lc[i, here] = old + cure[i, here] * source
            return carry

        if step == 0:
            lax.fori_loop(0, lx, update, 0)
        else:
            parts = 4
            each = lx // parts
            stores = []
            for part in range(parts):
                lax.fori_loop(part * each, (part + 1) * each, update, 0)
                for n, (source, target) in enumerate(((lu, out_t), (lc, out_c))):
                    store = pltpu.make_async_copy(
                        source.at[pl.ds(part * each, each)],
                        target.at[pl.ds(part * each, each)],
                        store_sem.at[n, part],
                    )
                    store.start()
                    stores.append(store)
            for store in stores:
                store.wait()
    for copy in started:
        copy.wait_send()


def per_device(nx, ny, ts, cs, tm, cm, al, ac, cf, bx, c2, by, ct, iz):
    lx, lyn, nz = al.shape
    f32 = jnp.float32
    vm = pltpu.VMEM
    tile = (lx, lyn, nz)
    hbm = pl.BlockSpec(memory_space=pl.ANY)
    smem = pl.BlockSpec(memory_space=pltpu.SMEM)
    vmem = pl.BlockSpec(memory_space=pltpu.VMEM)
    rx, ryn = lyn // nx, lx // ny
    scratch = (
        [vm(tile, f32)] * 7
        + [vm((lx + 2, lyn + 2 * MARGIN, nz), f32), vm((lx, 2 * nz), f32)]
        + [vm((lyn, nz), f32)] * 6
        + [vm((lx, 1, nz), f32)] * 2
        + [vm((2 * lyn + 2 * lx + 8, nz), f32)]
        + [vm((8, nz), f32), vm((nx, 8, nz), f32), vm((8, nz), f32), vm((ny, 8, nz), f32)]
        + [vm((nx, 8, nz), f32), vm((ny, 8, nz), f32)]
        + [vm((2, nx, 2, rx, nz), f32)] * 4
        + [vm((2, ny, 2, ryn, nz), f32)] * 4
        + [vm((2, 8, nz), f32), vm((2, ny, 8, nz), f32), vm((ny, 8, nz), f32)]
        + [vm((2, 8, nz), f32), vm((2, nx, 8, nz), f32), vm((nx, 8, nz), f32)]
        + [pltpu.SemaphoreType.DMA((6,)), pltpu.SemaphoreType.DMA((2, 4))]
        + [pltpu.SemaphoreType.DMA((7, nx))] * 2
        + [pltpu.SemaphoreType.DMA((7, ny))] * 2
    )
    return pl.pallas_call(
        functools.partial(kernel, nx, ny),
        out_shape=(jax.ShapeDtypeStruct(tile, f32), jax.ShapeDtypeStruct(tile, f32)),
        in_specs=[hbm] * 6 + [smem, smem, vmem, smem, vmem, vmem, vmem],
        out_specs=(hbm, hbm),
        scratch_shapes=scratch,
        compiler_params=pltpu.CompilerParams(
            collective_id=0, has_side_effects=True, vmem_limit_bytes=50 * 1024 * 1024
        ),
    )(ts, cs, tm, cm, al, ac, cf, bx, bx, c2, by, ct.reshape(1, -1), iz)


def solution(mesh):
    tile = P("gx", "gy", None)
    placed = (tile,) * 6 + (P("gx"), P("gx", None), P("gy"), P("gy", None), P(), P())
    return jax.shard_map(
        functools.partial(per_device, mesh.shape["gx"], mesh.shape["gy"]),
        mesh=mesh,
        in_specs=placed,
        out_specs=(tile, tile),
        check_vma=False,
    )
```

```python
import functools

import jax
import jax.numpy as jnp
from jax import lax
from jax.experimental import pallas as pl
from jax.experimental.pallas import tpu as pltpu
from jax.sharding import PartitionSpec as P

explicit_part = 2.0
heat_release = 100.0
cure_step = 0.5
arrhenius = 0.5
initial_rate = 0.1
highest = lax.Precision.HIGHEST
MESH = pl.DeviceIdType.MESH
MARGIN = 8


def dot(a, b):
    return jnp.dot(a, b, precision=highest, preferred_element_type=jnp.float32)


def reduced_coefficients(ends, coef, count):
    corner = None
    for k in range(count - 1):
        upper = ends[k, 3:4]
        if corner is not None:
            upper = upper + ends[k, 1:2] * ends[k, 2:3] * corner
        head = ends[k + 1, 0:1]
        bottom = 1.0 / (1.0 - upper * head)
        corner = upper * bottom
        right_next = ends[k + 1, 2:3]
        coef[k, 0:1] = bottom
        coef[k, 1:2] = corner
        coef[k, 2:3] = head * bottom
        coef[k, 3:4] = ends[k, 1:2]
        coef[k, 4:5] = bottom * right_next
        coef[k, 5:6] = corner * right_next


def reduced_solve(first, last, coef, count):
    tops, lows = [], []
    for k in range(count - 1):
        shifted = last(k)
        if k:
            shifted = shifted + coef[k, 3:4] * tops[-1]
        follow = first(k + 1)
        tops.append(coef[k, 0:1] * shifted + coef[k, 1:2] * follow)
        lows.append(coef[k, 2:3] * shifted + coef[k, 0:1] * follow)
    for k in range(count - 3, -1, -1):
        tops[k] = tops[k] + coef[k, 5:6] * lows[k + 1]
        lows[k] = lows[k] + coef[k, 4:5] * lows[k + 1]
    zero = jnp.zeros_like(first(0))
    return lows + [zero], [zero] + tops


def kernel(
    nx,
    ny,
    ts_hbm,
    cs_hbm,
    tm_hbm,
    cm_hbm,
    al_hbm,
    ac_hbm,
    cf_hbm,
    bx_hbm,
    c2_hbm,
    by_hbm,
    ct_hbm,
    iz_hbm,
    out_t,
    out_c,
    cf,
    bxs,
    bx,
    c2,
    by,
    ct,
    iz,
    lu,
    lc,
    t_mid,
    c_mid,
    t_start,
    c_start,
    g,
    mu,
    u,
    bycat,
    izcat,
    cya,
    cyb,
    wy0,
    wy1,
    ly,
    ry,
    tm_coef,
    tc_coef,
    zr,
    exs,
    exr,
    eys,
    eyr,
    coefx,
    coefy,
    xas,
    xar,
    xbs,
    xbr,
    yas,
    yar,
    ybs,
    ybr,
    eas,
    ear,
    eay,
    ebs,
    ebr,
    ebx,
    load_sem,
    store_sem,
    gx_send,
    gx_recv,
    gy_send,
    gy_recv,
):
    lx, lyn, nz = lu.shape
    rx = lyn // nx
    ryn = lx // ny
    mex = lax.axis_index("gx")
    mey = lax.axis_index("gy")
    sides = {"gx": (nx, mex, gx_send, gx_recv), "gy": (ny, mey, gy_send, gy_recv)}

    barrier = pltpu.get_barrier_semaphore()
    for axis, (count, me, _, _) in sides.items():
        for k in range(1, count):
            pl.semaphore_signal(
                barrier,
                inc=1,
                device_id={axis: lax.rem(me + k, count)},
                device_id_type=MESH,
            )

    loads = [
        pltpu.make_async_copy(source, target, load_sem.at[n])
        for n, (source, target) in enumerate(
            (
                (bx_hbm, bxs),
                (by_hbm, by),
                (al_hbm, lu),
                (bx_hbm, bx),
                (cf_hbm, cf),
                (c2_hbm, c2),
                (iz_hbm, iz),
                (ct_hbm, ct),
                (tm_hbm, t_mid),
                (cm_hbm, c_mid),
                (ac_hbm, lc),
                (ts_hbm, t_start),
                (cs_hbm, c_start),
            )
        )
    ]
    for load in loads:
        load.start()

    started = []

    def exchange(axis, kind, source, target):
        count, me, send, recv = sides[axis]
        copies = []
        for k in range(1, count):
            peer = lax.rem(me + k, count)
            copy = pltpu.make_async_remote_copy(
                src_ref=source(peer),
                dst_ref=target,
                send_sem=send.at[kind, k],
                recv_sem=recv.at[kind, k],
                device_id={axis: peer},
                device_id_type=MESH,
            )
            copy.start()
            copies.append(copy)
        started.extend(copies)
        return copies

    def arrive(copies):
        for copy in copies:
            copy.wait_recv()

    def row(value):
        return jnp.broadcast_to(value, (1, nz))

    wide = 4
    chunk = 16
    bf16 = jnp.bfloat16

    def prepare():
        def second_faces(j, carry):
            cya[pl.ds(j, 1)] = row(c2[j])
            cyb[pl.ds(j, 1)] = row(c2[j + 1])
            return carry

        lax.fori_loop(0, lyn, second_faces, 0, unroll=8)
        ly[...] = wy0[...] * s0
        ry[...] = wy1[...] * s1

        def eliminate(i, keep):
            partial = 1.0 + cf[i] * keep
            scale = 1.0 / (partial + cf[i + 1])
            tm_coef[i] = scale
            tc_coef[i] = cf[i + 1] * scale
            return partial * scale

        lax.fori_loop(0, lx, eliminate, jnp.ones((1, nz), jnp.float32), unroll=4)
        matrix = by[...]
        part0 = matrix.astype(bf16)
        rest = matrix - part0.astype(jnp.float32)
        part1 = rest.astype(bf16)
        part2 = (rest - part1.astype(jnp.float32)).astype(bf16)
        for n, part in enumerate((part0, part1, part2)):
            bycat[n * lyn : (n + 1) * lyn] = jnp.concatenate([part, part], axis=1)
        matrix = iz[...]
        part0 = matrix.astype(bf16)
        izcat[0] = part0
        izcat[1] = (matrix - part0.astype(jnp.float32)).astype(bf16)

    loads[0].wait()
    loads[1].wait()
    wy0[...] = jnp.broadcast_to(by[:, 0:1], (lyn, nz))
    wy1[...] = jnp.broadcast_to(by[:, lyn - 1 : lyn], (lyn, nz))
    eas[...] = jnp.zeros_like(eas)
    ebs[...] = jnp.zeros_like(ebs)
    zr[...] = jnp.zeros_like(zr)
    exs[...] = jnp.zeros_like(exs)
    eys[...] = jnp.zeros_like(eys)
    empty = jnp.zeros((lyn, nz), jnp.float32)

    def fold(value):
        return jnp.sum(value.reshape(-1, 8, nz), axis=0)

    loads[2].wait()

    def tips(i, carry):
        first, last = carry
        slab = lu[i]
        u[0, i] = fold(slab * wy0[...])
        u[1, i] = fold(slab * wy1[...])
        return first + bxs[i, 0] * slab, last + bxs[i, lx - 1] * slab

    first, last = lax.fori_loop(0, lx, tips, (empty, empty))

    for step in range(2):
        temper, cure = ((t_mid, c_mid), (t_start, c_start))[step]
        tip_x = dot(by[...], jnp.concatenate([first, last], axis=1))
        for d in range(nx):
            xas[step, d, 0] = tip_x[d * rx : (d + 1) * rx, 0:nz]
            xas[step, d, 1] = tip_x[d * rx : (d + 1) * rx, nz:]
        if step == 0:
            for n in (3, 4, 5):
                loads[n].wait()
            a0, a1 = cf[0], cf[lx]
            exs[0:1] = row(a0 * bxs[0, 0])
            exs[1:2] = row(a0 * bxs[0, lx - 1])
            exs[2:3] = row(a1 * bxs[lx - 1, 0])
            exs[3:4] = row(a1 * bxs[lx - 1, lx - 1])
            s0, s1 = c2[0], c2[lyn]
            eys[0:1] = row(by[0:1, 0:1]) * s0
            eys[1:2] = row(by[0:1, lyn - 1 : lyn]) * s0
            eys[2:3] = row(by[lyn - 1 : lyn, 0:1]) * s1
            eys[3:4] = row(by[lyn - 1 : lyn, lyn - 1 : lyn]) * s1
            pl.semaphore_wait(barrier, nx + ny - 2)
        out_xa = exchange("gx", 1 + 3 * step, lambda peer: xas.at[step, peer], xar.at[step, mex])
        eas[step, 0:1] = tip_x[0:1, 0:nz]
        eas[step, 1:2] = tip_x[0:1, nz:]
        eas[step, 2:3] = tip_x[lyn - 1 : lyn, 0:nz]
        eas[step, 3:4] = tip_x[lyn - 1 : lyn, nz:]
        out_ea = exchange("gy", 3 + 3 * step, lambda peer: eas.at[step], ear.at[step, mey])
        tip_y = dot(
            bx[...], jnp.concatenate([jnp.sum(u[0], axis=1), jnp.sum(u[1], axis=1)], axis=1)
        )
        for d in range(ny):
            yas[step, d, 0] = tip_y[d * ryn : (d + 1) * ryn, 0:nz]
            yas[step, d, 1] = tip_y[d * ryn : (d + 1) * ryn, nz:]
        out_ya = exchange("gy", 1 + 3 * step, lambda peer: yas.at[step, peer], yar.at[step, mey])
        xar[step, mex] = xas[step, mex]
        yar[step, mey] = yas[step, mey]
        ear[step, mey] = eas[step]

        if step == 0:
            ends_x = exchange("gx", 0, lambda peer: exs, exr.at[mex])
            ends_y = exchange("gy", 0, lambda peer: eys, eyr.at[mey])
            exr[mex] = exs[...]
            eyr[mey] = eys[...]
            loads[6].wait()
            loads[7].wait()
            prepare()
            face_low = ct[:, 0:nz]
            face_high = ct[:, 1 : nz + 1]

        def through(n, carry):
            block = lu[pl.ds(n * wide, wide)].reshape(wide * lyn, nz)
            high = block.astype(bf16)
            low = (block - high.astype(jnp.float32)).astype(bf16)
            done = (
                jnp.dot(high, izcat[1], preferred_element_type=jnp.float32)
                + jnp.dot(low, izcat[0], preferred_element_type=jnp.float32)
                + jnp.dot(high, izcat[0], preferred_element_type=jnp.float32)
            )
            g[pl.ds(n * wide, wide)] = done.reshape(wide, lyn, nz)
            return carry

        lax.fori_loop(0, lx // wide, through, 0, unroll=2)

        def forward(i, before):
            slab = g[i]
            high = slab.astype(bf16)
            low = (slab - high.astype(jnp.float32)).astype(bf16)
            stacked = jnp.dot(
                bycat[...],
                jnp.concatenate([high, low], axis=0),
                preferred_element_type=jnp.float32,
            )
            solved = (stacked[2 * lyn :] + stacked[lyn : 2 * lyn]) + stacked[0:lyn]
            value = (solved + cf[i] * before) * tm_coef[i]
            g[i] = value
            return value

        lax.fori_loop(0, lx, forward, empty, unroll=4)

        if step == 0:
            arrive(ends_x)
            arrive(ends_y)
            reduced_coefficients(exr, coefx, nx)
            reduced_coefficients(eyr, coefy, ny)
        arrive(out_xa)
        lows, tops = reduced_solve(
            lambda k: xar[step, k, 0], lambda k: xar[step, k, 1], coefx, nx
        )
        for d in range(nx):
            xbs[step, d, 0] = lows[d]
            xbs[step, d, 1] = tops[d]
        out_xb = exchange("gx", 2 + 3 * step, lambda peer: xbs.at[step, peer], xbr.at[step, mex])
        arrive(out_ea)
        lows, tops = reduced_solve(
            lambda k: ear[step, k, 0:2], lambda k: ear[step, k, 2:4], coefy, ny
        )
        for d in range(ny):
            eay[d, 0:2] = lows[d]
            eay[d, 2:4] = tops[d]
        edge = eay[mey]
        ebs[step, 0:1] = edge[0:1]
        ebs[step, 1:2] = edge[2:3]
        ebs[step, 2:3] = edge[1:2]
        ebs[step, 3:4] = edge[3:4]
        out_eb = exchange("gx", 3 + 3 * step, lambda peer: ebs.at[step], ebr.at[step, mex])
        arrive(out_ya)
        lows, tops = reduced_solve(
            lambda k: yar[step, k, 0], lambda k: yar[step, k, 1], coefy, ny
        )
        for d in range(ny):
            ybs[step, d, 0] = lows[d]
            ybs[step, d, 1] = tops[d]
        out_yb = exchange("gy", 2 + 3 * step, lambda peer: ybs.at[step, peer], ybr.at[step, mey])
        xbr[step, mex] = xbs[step, mex]
        ybr[step, mey] = ybs[step, mey]
        ebr[step, mex] = ebs[step]

        inside = slice(MARGIN, MARGIN + lyn)

        def backward(n, after):
            i = lx - 1 - n
            value = g[i] + tc_coef[i] * after
            mu[i + 1, inside] = value
            return value

        lax.fori_loop(0, lx, backward, empty, unroll=4)

        if step == 0:
            for n in (8, 9, 10):
                loads[n].wait()
        else:
            loads[11].wait()
            loads[12].wait()

        def rates(i, carry):
            heating = jnp.exp(arrhenius * temper[i])
            value = cure[i]
            remain = 1.0 - value
            grown = initial_rate + value
            temper[i] = arrhenius * (heating * grown * remain * remain)
            cure[i] = heating * (remain * remain - 2.0 * grown * remain)
            return carry

        lax.fori_loop(0, lx, rates, 0, unroll=2)

        arrive(out_eb)
        lows, tops = reduced_solve(
            lambda k: ebr[step, k, 0:2], lambda k: ebr[step, k, 2:4], coefx, nx
        )
        for d in range(nx):
            ebx[d, 0:2] = lows[d]
            ebx[d, 2:4] = tops[d]
        arrive(out_xb)
        arrive(out_yb)
        for d in range(nx):
            zr[d * rx : (d + 1) * rx] = xbr[step, d, 0]
            zr[lyn + d * rx : lyn + (d + 1) * rx] = xbr[step, d, 1]
        base = 2 * lyn
        for d in range(ny):
            zr[base + d * ryn : base + (d + 1) * ryn] = ybr[step, d, 0]
            zr[base + lx + d * ryn : base + lx + (d + 1) * ryn] = ybr[step, d, 1]
        corner = base + 2 * lx
        zr[corner : corner + 4] = ebx[mex, 0:4]
        zr[...] = dot(zr[...], iz[...])
        next_next = zr[corner : corner + 1]
        next_prev = zr[corner + 1 : corner + 2]
        prev_next = zr[corner + 2 : corner + 3]
        prev_prev = zr[corner + 3 : corner + 4]
        mu[lx + 1, inside] = zr[0:lyn] + ly[...] * next_prev + ry[...] * next_next
        mu[0, inside] = zr[lyn : 2 * lyn] + ly[...] * prev_prev + ry[...] * prev_next

        def correct(i, carry):
            left = a0 * bxs[0, i]
            right = a1 * bxs[lx - 1, i]
            y_next = zr[pl.ds(base + i, 1)]
            y_prev = zr[pl.ds(base + lx + i, 1)]
            mu[i + 1, inside] = (
                mu[i + 1, inside]
                + left * mu[0, inside]
                + right * mu[lx + 1, inside]
                + ly[...] * y_prev
                + ry[...] * y_next
            )
            mu[i + 1, MARGIN - 1 : MARGIN] = y_prev + left * prev_prev + right * next_prev
            mu[i + 1, MARGIN + lyn : MARGIN + lyn + 1] = (
                y_next + left * prev_next + right * next_next
            )
            return carry

        lax.fori_loop(0, lx, correct, 0, unroll=2)

        lane = lax.broadcasted_iota(jnp.int32, (chunk, nz), 1)
        stores = []
        firsts, lasts = [], []
        for part, y in enumerate(range(0, lyn, chunk)):
            here = slice(y, y + chunk)
            start = MARGIN + y

            def update(i, carry):
                lower, value, first, last = carry
                upper = mu[i + 2, start : start + chunk]
                below = jnp.where(lane == 0, 0.0, pltpu.roll(value, 1, 1))
                above = jnp.where(lane == nz - 1, 0.0, pltpu.roll(value, nz - 1, 1))
                kick = (
                    cf[i] * (value - lower)
                    + cf[i + 1] * (value - upper)
                    + cya[here] * (value - mu[i + 1, start - 1 : start + chunk - 1])
                    + cyb[here] * (value - mu[i + 1, start + 1 : start + chunk + 1])
                    + face_low * (value - below)
                    + face_high * (value - above)
                )
                old = lc[i, here]
                source = heat_release * value + cure_step * old
                new = lu[i, here] - explicit_part * kick + temper[i, here] * source
                lu[i, here] = new
                lc[i, here] = old + cure[i, here] * source
                if step == 0:
                    first = first + bxs[i, 0] * new
                    last = last + bxs[i, lx - 1] * new
                    for n, weight in enumerate((wy0, wy1)):
                        folded = fold(new * weight[here])
                        u[n, i] = folded if part == 0 else u[n, i] + folded
                return upper, value, first, last

            def ordered(i, carry):
                upper, value, first, last = update(i, carry)
                return value, upper, first, last

            none = jnp.zeros((chunk, nz), jnp.float32)
            begin = (mu[0, start : start + chunk], mu[1, start : start + chunk], none, none)
            _, _, first, last = lax.fori_loop(0, lx, ordered, begin, unroll=2)
            firsts.append(first)
            lasts.append(last)
            if step == 1:
                for n, (source, target) in enumerate(((lu, out_t), (lc, out_c))):
                    store = pltpu.make_async_copy(
                        source.at[:, pl.ds(y, chunk)],
                        target.at[:, pl.ds(y, chunk)],
                        store_sem.at[n, part],
                    )
                    store.start()
                    stores.append(store)
        first = jnp.concatenate(firsts, axis=0)
        last = jnp.concatenate(lasts, axis=0)
        for store in stores:
            store.wait()
    for copy in started:
        copy.wait_send()


def per_device(nx, ny, ts, cs, tm, cm, al, ac, cf, bx, c2, by, ct, iz):
    lx, lyn, nz = al.shape
    f32 = jnp.float32
    vm = pltpu.VMEM
    tile = (lx, lyn, nz)
    hbm = pl.BlockSpec(memory_space=pltpu.HBM)
    sm = pltpu.SMEM
    rx, ryn = lyn // nx, lx // ny
    scratch = (
        [sm(cf.shape, f32), sm(bx.shape, f32), vm(bx.shape, f32), sm(c2.shape, f32)]
        + [vm(by.shape, f32), vm((1, nz + 1), f32), vm(iz.shape, f32)]
        + [vm(tile, f32)] * 7
        + [vm((lx + 2, lyn + 2 * MARGIN, nz), f32), vm((2, lx, 8, nz), f32)]
        + [vm((3 * lyn, 2 * lyn), jnp.bfloat16), vm((2, nz, nz), jnp.bfloat16)]
        + [vm((lyn, nz), f32)] * 6
        + [vm((lx, 1, nz), f32)] * 2
        + [vm((2 * lyn + 2 * lx + 8, nz), f32)]
        + [vm((8, nz), f32), vm((nx, 8, nz), f32), vm((8, nz), f32), vm((ny, 8, nz), f32)]
        + [vm((nx, 8, nz), f32), vm((ny, 8, nz), f32)]
        + [vm((2, nx, 2, rx, nz), f32)] * 4
        + [vm((2, ny, 2, ryn, nz), f32)] * 4
        + [vm((2, 8, nz), f32), vm((2, ny, 8, nz), f32), vm((ny, 8, nz), f32)]
        + [vm((2, 8, nz), f32), vm((2, nx, 8, nz), f32), vm((nx, 8, nz), f32)]
        + [pltpu.SemaphoreType.DMA((13,)), pltpu.SemaphoreType.DMA((2, lyn // 16))]
        + [pltpu.SemaphoreType.DMA((7, nx))] * 2
        + [pltpu.SemaphoreType.DMA((7, ny))] * 2
    )
    return pl.pallas_call(
        functools.partial(kernel, nx, ny),
        out_shape=(jax.ShapeDtypeStruct(tile, f32), jax.ShapeDtypeStruct(tile, f32)),
        in_specs=[hbm] * 12,
        out_specs=(hbm, hbm),
        scratch_shapes=scratch,
        compiler_params=pltpu.CompilerParams(
            collective_id=0, has_side_effects=True, vmem_limit_bytes=56 * 1024 * 1024
        ),
    )(ts, cs, tm, cm, al, ac, cf, bx, c2, by, ct.reshape(1, -1), iz)


def solution(mesh):
    tile = P("gx", "gy", None)
    placed = (tile,) * 6 + (P("gx"), P("gx", None), P("gy"), P("gy", None), P(), P())
    return jax.shard_map(
        functools.partial(per_device, mesh.shape["gx"], mesh.shape["gy"]),
        mesh=mesh,
        in_specs=placed,
        out_specs=(tile, tile),
        check_vma=False,
    )
```

```python
import functools

import jax
import jax.numpy as jnp
from jax import lax
from jax.experimental import pallas as pl
from jax.experimental.pallas import tpu as pltpu
from jax.sharding import PartitionSpec as P

explicit_part = 2.0
heat_release = 100.0
cure_step = 0.5
arrhenius = 0.5
initial_rate = 0.1
highest = lax.Precision.HIGHEST
MESH = pl.DeviceIdType.MESH
MARGIN = 8


def dot(a, b):
    return jnp.dot(a, b, precision=highest, preferred_element_type=jnp.float32)


def reduced_coefficients(ends, coef, count):
    corner = None
    for k in range(count - 1):
        upper = ends[k, 3:4]
        if corner is not None:
            upper = upper + ends[k, 1:2] * ends[k, 2:3] * corner
        head = ends[k + 1, 0:1]
        bottom = 1.0 / (1.0 - upper * head)
        corner = upper * bottom
        right_next = ends[k + 1, 2:3]
        coef[k, 0:1] = bottom
        coef[k, 1:2] = corner
        coef[k, 2:3] = head * bottom
        coef[k, 3:4] = ends[k, 1:2]
        coef[k, 4:5] = bottom * right_next
        coef[k, 5:6] = corner * right_next


def reduced_solve(first, last, coef, count):
    tops, lows = [], []
    for k in range(count - 1):
        shifted = last(k)
        if k:
            shifted = shifted + coef[k, 3:4] * tops[-1]
        follow = first(k + 1)
        tops.append(coef[k, 0:1] * shifted + coef[k, 1:2] * follow)
        lows.append(coef[k, 2:3] * shifted + coef[k, 0:1] * follow)
    for k in range(count - 3, -1, -1):
        tops[k] = tops[k] + coef[k, 5:6] * lows[k + 1]
        lows[k] = lows[k] + coef[k, 4:5] * lows[k + 1]
    zero = jnp.zeros_like(first(0))
    return lows + [zero], [zero] + tops


def kernel(
    nx,
    ny,
    ts_hbm,
    cs_hbm,
    tm_hbm,
    cm_hbm,
    al_hbm,
    ac_hbm,
    cf_hbm,
    bx_hbm,
    c2_hbm,
    by_hbm,
    ct_hbm,
    iz_hbm,
    out_t,
    out_c,
    cf,
    bxs,
    bx,
    c2,
    by,
    ct,
    iz,
    lu,
    lc,
    t_mid,
    c_mid,
    t_start,
    c_start,
    lu_second,
    lc_second,
    rate_t,
    rate_c,
    g,
    h,
    x_next,
    x_prev,
    mu,
    u,
    bycat,
    izcat,
    cya,
    cyb,
    wy0,
    wy1,
    ly,
    ry,
    tm_coef,
    tc_coef,
    zr,
    exs,
    exr,
    eys,
    eyr,
    coefx,
    coefy,
    xas,
    xar,
    xbs,
    xbr,
    yas,
    yar,
    ybs,
    ybr,
    eas,
    ear,
    eay,
    ebs,
    ebr,
    ebx,
    load_sem,
    store_sem,
    gx_send,
    gx_recv,
    gy_send,
    gy_recv,
):
    lx, lyn, nz = lu.shape
    rx = lyn // nx
    ryn = lx // ny
    mex = lax.axis_index("gx")
    mey = lax.axis_index("gy")
    sides = {"gx": (nx, mex, gx_send, gx_recv), "gy": (ny, mey, gy_send, gy_recv)}

    barrier = pltpu.get_barrier_semaphore()
    for axis, (count, me, _, _) in sides.items():
        for k in range(1, count):
            pl.semaphore_signal(
                barrier,
                inc=1,
                device_id={axis: lax.rem(me + k, count)},
                device_id_type=MESH,
            )

    loads = [
        pltpu.make_async_copy(source, target, load_sem.at[n])
        for n, (source, target) in enumerate(
            (
                (bx_hbm, bxs),
                (by_hbm, by),
                (al_hbm, lu),
                (bx_hbm, bx),
                (cf_hbm, cf),
                (c2_hbm, c2),
                (iz_hbm, iz),
                (ct_hbm, ct),
                (tm_hbm, t_mid),
                (cm_hbm, c_mid),
                (ac_hbm, lc),
                (ts_hbm, t_start),
                (cs_hbm, c_start),
            )
        )
    ]
    for load in loads:
        load.start()

    started = []

    def exchange(axis, kind, source, target):
        count, me, send, recv = sides[axis]
        copies = []
        for k in range(1, count):
            peer = lax.rem(me + k, count)
            copy = pltpu.make_async_remote_copy(
                src_ref=source(peer),
                dst_ref=target,
                send_sem=send.at[kind, k],
                recv_sem=recv.at[kind, k],
                device_id={axis: peer},
                device_id_type=MESH,
            )
            copy.start()
            copies.append(copy)
        started.extend(copies)
        return copies

    def arrive(copies):
        for copy in copies:
            copy.wait_recv()

    def row(value):
        return jnp.broadcast_to(value, (1, nz))

    wide = 4
    chunk = 32
    bf16 = jnp.bfloat16

    def prepare():
        def second_faces(j, carry):
            cya[pl.ds(j, 1)] = row(c2[j])
            cyb[pl.ds(j, 1)] = row(c2[j + 1])
            return carry

        lax.fori_loop(0, lyn, second_faces, 0, unroll=8)
        ly[...] = wy0[...] * s0
        ry[...] = wy1[...] * s1

        def eliminate(i, keep):
            partial = 1.0 + cf[i] * keep
            scale = 1.0 / (partial + cf[i + 1])
            tm_coef[i] = scale
            tc_coef[i] = cf[i + 1] * scale
            return partial * scale

        lax.fori_loop(0, lx, eliminate, jnp.ones((1, nz), jnp.float32), unroll=4)
        matrix = by[...]
        part0 = matrix.astype(bf16)
        rest = matrix - part0.astype(jnp.float32)
        part1 = rest.astype(bf16)
        part2 = (rest - part1.astype(jnp.float32)).astype(bf16)
        for n, part in enumerate((part0, part1, part2)):
            bycat[n * lyn : (n + 1) * lyn] = jnp.concatenate([part, part], axis=1)
        matrix = iz[...]
        part0 = matrix.astype(bf16)
        izcat[0] = part0
        izcat[1] = (matrix - part0.astype(jnp.float32)).astype(bf16)

    loads[0].wait()
    loads[1].wait()
    wy0[...] = jnp.broadcast_to(by[:, 0:1], (lyn, nz))
    wy1[...] = jnp.broadcast_to(by[:, lyn - 1 : lyn], (lyn, nz))
    eas[...] = jnp.zeros_like(eas)
    ebs[...] = jnp.zeros_like(ebs)
    zr[...] = jnp.zeros_like(zr)
    exs[...] = jnp.zeros_like(exs)
    eys[...] = jnp.zeros_like(eys)
    empty = jnp.zeros((lyn, nz), jnp.float32)

    def fold(value):
        return jnp.sum(value.reshape(-1, 8, nz), axis=0)

    loads[2].wait()

    def tips(i, carry):
        first, last = carry
        slab = lu[i]
        u[0, 0, i] = fold(slab * wy0[...])
        u[1, 0, i] = fold(slab * wy1[...])
        return first + bxs[i, 0] * slab, last + bxs[i, lx - 1] * slab

    first, last = lax.fori_loop(0, lx, tips, (empty, empty), unroll=4)

    for step in range(2):
        temper, cure = ((t_mid, c_mid), (t_start, c_start))[step]
        lu_now, lc_now = ((lu, lc), (lu_second, lc_second))[step]
        lu_then, lc_then = ((lu_second, lc_second), (lu, lc))[step]
        tip_x = dot(by[...], jnp.concatenate([first, last], axis=1))
        for d in range(nx):
            xas[step, d, 0] = tip_x[d * rx : (d + 1) * rx, 0:nz]
            xas[step, d, 1] = tip_x[d * rx : (d + 1) * rx, nz:]
        if step == 0:
            for n in (3, 4, 5):
                loads[n].wait()
            a0, a1 = cf[0], cf[lx]
            exs[0:1] = row(a0 * bxs[0, 0])
            exs[1:2] = row(a0 * bxs[0, lx - 1])
            exs[2:3] = row(a1 * bxs[lx - 1, 0])
            exs[3:4] = row(a1 * bxs[lx - 1, lx - 1])
            s0, s1 = c2[0], c2[lyn]
            eys[0:1] = row(by[0:1, 0:1]) * s0
            eys[1:2] = row(by[0:1, lyn - 1 : lyn]) * s0
            eys[2:3] = row(by[lyn - 1 : lyn, 0:1]) * s1
            eys[3:4] = row(by[lyn - 1 : lyn, lyn - 1 : lyn]) * s1
            pl.semaphore_wait(barrier, nx + ny - 2)
        out_xa = exchange("gx", 1 + 3 * step, lambda peer: xas.at[step, peer], xar.at[step, mex])
        eas[step, 0:1] = tip_x[0:1, 0:nz]
        eas[step, 1:2] = tip_x[0:1, nz:]
        eas[step, 2:3] = tip_x[lyn - 1 : lyn, 0:nz]
        eas[step, 3:4] = tip_x[lyn - 1 : lyn, nz:]
        out_ea = exchange("gy", 3 + 3 * step, lambda peer: eas.at[step], ear.at[step, mey])
        folded = [u[n, 0] if step == 0 else u[n, 0] + u[n, 1] for n in range(2)]
        tip_y = dot(bx[...], jnp.concatenate([jnp.sum(f, axis=1) for f in folded], axis=1))
        for d in range(ny):
            yas[step, d, 0] = tip_y[d * ryn : (d + 1) * ryn, 0:nz]
            yas[step, d, 1] = tip_y[d * ryn : (d + 1) * ryn, nz:]
        out_ya = exchange("gy", 1 + 3 * step, lambda peer: yas.at[step, peer], yar.at[step, mey])
        xar[step, mex] = xas[step, mex]
        yar[step, mey] = yas[step, mey]
        ear[step, mey] = eas[step]

        if step == 0:
            ends_x = exchange("gx", 0, lambda peer: exs, exr.at[mex])
            ends_y = exchange("gy", 0, lambda peer: eys, eyr.at[mey])
            exr[mex] = exs[...]
            eyr[mey] = eys[...]
            loads[6].wait()
            loads[7].wait()
            prepare()
            face_low = ct[0:nz].reshape(1, nz)
            face_high = ct[1 : nz + 1].reshape(1, nz)

        def through(n, carry):
            block = lu_now[pl.ds(n * wide, wide)].reshape(wide * lyn, nz)
            high = block.astype(bf16)
            low = (block - high.astype(jnp.float32)).astype(bf16)
            done = (
                jnp.dot(high, izcat[1], preferred_element_type=jnp.float32)
                + jnp.dot(low, izcat[0], preferred_element_type=jnp.float32)
                + jnp.dot(high, izcat[0], preferred_element_type=jnp.float32)
            )
            g[pl.ds(n * wide, wide)] = done.reshape(wide, lyn, nz)
            return carry

        lax.fori_loop(0, lx // wide, through, 0, unroll=2)

        def forward(n, before):
            solved = []
            for k in range(wide):
                slab = g[n * wide + k]
                high = slab.astype(bf16)
                low = (slab - high.astype(jnp.float32)).astype(bf16)
                stacked = jnp.dot(
                    bycat[...],
                    jnp.concatenate([high, low], axis=0),
                    preferred_element_type=jnp.float32,
                )
                solved.append((stacked[2 * lyn :] + stacked[lyn : 2 * lyn]) + stacked[0:lyn])
            for k in range(wide):
                i = n * wide + k
                before = (solved[k] + cf[i] * before) * tm_coef[i]
                h[i] = before
            return before

        lax.fori_loop(0, lx // wide, forward, empty)

        if step == 0:
            arrive(ends_x)
            arrive(ends_y)
            reduced_coefficients(exr, coefx, nx)
            reduced_coefficients(eyr, coefy, ny)
        arrive(out_xa)
        lows, tops = reduced_solve(
            lambda k: xar[step, k, 0], lambda k: xar[step, k, 1], coefx, nx
        )
        for d in range(nx):
            xbs[step, d, 0] = lows[d]
            xbs[step, d, 1] = tops[d]
        out_xb = exchange("gx", 2 + 3 * step, lambda peer: xbs.at[step, peer], xbr.at[step, mex])
        arrive(out_ea)
        lows, tops = reduced_solve(
            lambda k: ear[step, k, 0:2], lambda k: ear[step, k, 2:4], coefy, ny
        )
        for d in range(ny):
            eay[d, 0:2] = lows[d]
            eay[d, 2:4] = tops[d]
        edge = eay[mey]
        ebs[step, 0:1] = edge[0:1]
        ebs[step, 1:2] = edge[2:3]
        ebs[step, 2:3] = edge[1:2]
        ebs[step, 3:4] = edge[3:4]
        out_eb = exchange("gx", 3 + 3 * step, lambda peer: ebs.at[step], ebr.at[step, mex])
        arrive(out_ya)
        lows, tops = reduced_solve(
            lambda k: yar[step, k, 0], lambda k: yar[step, k, 1], coefy, ny
        )
        for d in range(ny):
            ybs[step, d, 0] = lows[d]
            ybs[step, d, 1] = tops[d]
        out_yb = exchange("gy", 2 + 3 * step, lambda peer: ybs.at[step, peer], ybr.at[step, mey])
        xbr[step, mex] = xbs[step, mex]
        ybr[step, mey] = ybs[step, mey]
        ebr[step, mex] = ebs[step]

        inside = slice(MARGIN, MARGIN + lyn)

        def backward(n, after):
            i = lx - 1 - n
            value = h[i] + tc_coef[i] * after
            g[i] = value
            return value

        lax.fori_loop(0, lx, backward, empty, unroll=4)

        if step == 0:
            for n in (8, 9, 10):
                loads[n].wait()
        else:
            loads[11].wait()
            loads[12].wait()

        def rates(i, carry):
            heating = jnp.exp(arrhenius * temper[i])
            value = cure[i]
            remain = 1.0 - value
            grown = initial_rate + value
            rate_t[i] = arrhenius * (heating * grown * remain * remain)
            rate_c[i] = heating * (remain * remain - 2.0 * grown * remain)
            return carry

        lax.fori_loop(0, lx, rates, 0, unroll=2)

        arrive(out_eb)
        lows, tops = reduced_solve(
            lambda k: ebr[step, k, 0:2], lambda k: ebr[step, k, 2:4], coefx, nx
        )
        for d in range(nx):
            ebx[d, 0:2] = lows[d]
            ebx[d, 2:4] = tops[d]
        arrive(out_xb)
        arrive(out_yb)
        for d in range(nx):
            zr[d * rx : (d + 1) * rx] = xbr[step, d, 0]
            zr[lyn + d * rx : lyn + (d + 1) * rx] = xbr[step, d, 1]
        base = 2 * lyn
        for d in range(ny):
            zr[base + d * ryn : base + (d + 1) * ryn] = ybr[step, d, 0]
            zr[base + lx + d * ryn : base + lx + (d + 1) * ryn] = ybr[step, d, 1]
        corner = base + 2 * lx
        zr[corner : corner + 4] = ebx[mex, 0:4]
        zr[...] = dot(zr[...], iz[...])
        next_next = zr[corner : corner + 1]
        next_prev = zr[corner + 1 : corner + 2]
        prev_next = zr[corner + 2 : corner + 3]
        prev_prev = zr[corner + 3 : corner + 4]
        value = zr[0:lyn] + ly[...] * next_prev + ry[...] * next_next
        x_next[...] = value
        mu[lx + 1, inside] = value
        value = zr[lyn : 2 * lyn] + ly[...] * prev_prev + ry[...] * prev_next
        x_prev[...] = value
        mu[0, inside] = value

        def correct(i, carry):
            left = a0 * bxs[0, i]
            right = a1 * bxs[lx - 1, i]
            y_next = zr[pl.ds(base + i, 1)]
            y_prev = zr[pl.ds(base + lx + i, 1)]
            mu[i + 1, inside] = (
                g[i]
                + left * x_prev[...]
                + right * x_next[...]
                + ly[...] * y_prev
                + ry[...] * y_next
            )
            mu[i + 1, MARGIN - 1 : MARGIN] = y_prev + left * prev_prev + right * next_prev
            mu[i + 1, MARGIN + lyn : MARGIN + lyn + 1] = (
                y_next + left * prev_next + right * next_next
            )
            return carry

        lax.fori_loop(0, lx, correct, 0, unroll=4)

        lane = lax.broadcasted_iota(jnp.int32, (chunk, nz), 1)
        stores = []
        firsts, lasts = [], []
        for part, y in enumerate(range(0, lyn, chunk)):
            here = slice(y, y + chunk)
            start = MARGIN + y

            def update(i, carry):
                first, last = carry
                value = mu[i + 1, start : start + chunk]
                below = jnp.where(lane == 0, 0.0, pltpu.roll(value, 1, 1))
                above = jnp.where(lane == nz - 1, 0.0, pltpu.roll(value, nz - 1, 1))
                kick = (
                    cf[i] * (value - mu[i, start : start + chunk])
                    + cf[i + 1] * (value - mu[i + 2, start : start + chunk])
                    + cya[here] * (value - mu[i + 1, start - 1 : start + chunk - 1])
                    + cyb[here] * (value - mu[i + 1, start + 1 : start + chunk + 1])
                    + face_low * (value - below)
                    + face_high * (value - above)
                )
                old = lc_now[i, here]
                source = heat_release * value + cure_step * old
                new = lu_now[i, here] - explicit_part * kick + rate_t[i, here] * source
                lu_then[i, here] = new
                lc_then[i, here] = old + rate_c[i, here] * source
                if step == 0:
                    first = first + bxs[i, 0] * new
                    last = last + bxs[i, lx - 1] * new
                    u[0, part, i] = fold(new * wy0[here])
                    u[1, part, i] = fold(new * wy1[here])
                return first, last

            none = jnp.zeros((chunk, nz), jnp.float32)
            first, last = lax.fori_loop(0, lx, update, (none, none), unroll=4)
            firsts.append(first)
            lasts.append(last)
            if step == 1:
                for n, (source, target) in enumerate(((lu, out_t), (lc, out_c))):
                    store = pltpu.make_async_copy(
                        source.at[:, pl.ds(y, chunk)],
                        target.at[:, pl.ds(y, chunk)],
                        store_sem.at[n, part],
                    )
                    store.start()
                    stores.append(store)
        first = jnp.concatenate(firsts, axis=0)
        last = jnp.concatenate(lasts, axis=0)
        for store in stores:
            store.wait()
    for copy in started:
        copy.wait_send()


def hand_out(first, second, out_first, out_second, sem):
    half = first.shape[0] // 2
    copies = [
        pltpu.make_async_copy(
            source.at[pl.ds(part * half, half)], target.at[pl.ds(part * half, half)], sem.at[n, part]
        )
        for n, (source, target) in enumerate(((first, out_first), (second, out_second)))
        for part in range(2)
    ]
    for copy in copies:
        copy.start()
    for copy in copies:
        copy.wait()


def per_device(nx, ny, ts, cs, tm, cm, al, ac, cf, bx, c2, by, ct, iz):
    lx, lyn, nz = al.shape
    f32 = jnp.float32
    vm = pltpu.VMEM
    tile = (lx, lyn, nz)
    anywhere = pl.BlockSpec(memory_space=pl.ANY)
    hbm = pl.BlockSpec(memory_space=pltpu.HBM)
    sm = pltpu.SMEM
    rx, ryn = lyn // nx, lx // ny
    scratch = (
        [sm(cf.shape, f32), sm(bx.shape, f32), vm(bx.shape, f32), sm(c2.shape, f32)]
        + [vm(by.shape, f32), vm((nz + 1,), f32), vm(iz.shape, f32)]
        + [vm(tile, f32)] * 12
        + [vm((lyn, nz), f32)] * 2
        + [vm((lx + 2, lyn + 2 * MARGIN, nz), f32), vm((2, 2, lx, 8, nz), f32)]
        + [vm((3 * lyn, 2 * lyn), jnp.bfloat16), vm((2, nz, nz), jnp.bfloat16)]
        + [vm((lyn, nz), f32)] * 6
        + [vm((lx, 1, nz), f32)] * 2
        + [vm((2 * lyn + 2 * lx + 8, nz), f32)]
        + [vm((8, nz), f32), vm((nx, 8, nz), f32), vm((8, nz), f32), vm((ny, 8, nz), f32)]
        + [vm((nx, 8, nz), f32), vm((ny, 8, nz), f32)]
        + [vm((2, nx, 2, rx, nz), f32)] * 4
        + [vm((2, ny, 2, ryn, nz), f32)] * 4
        + [vm((2, 8, nz), f32), vm((2, ny, 8, nz), f32), vm((ny, 8, nz), f32)]
        + [vm((2, 8, nz), f32), vm((2, nx, 8, nz), f32), vm((nx, 8, nz), f32)]
        + [pltpu.SemaphoreType.DMA((13,)), pltpu.SemaphoreType.DMA((2, lyn // 32))]
        + [pltpu.SemaphoreType.DMA((7, nx))] * 2
        + [pltpu.SemaphoreType.DMA((7, ny))] * 2
    )
    results = pl.pallas_call(
        functools.partial(kernel, nx, ny),
        out_shape=(jax.ShapeDtypeStruct(tile, f32), jax.ShapeDtypeStruct(tile, f32)),
        in_specs=[hbm] * 12,
        out_specs=(anywhere, anywhere),
        scratch_shapes=scratch,
        compiler_params=pltpu.CompilerParams(
            collective_id=0, has_side_effects=True, vmem_limit_bytes=60 * 1024 * 1024
        ),
    )(ts, cs, tm, cm, al, ac, cf, bx, c2, by, ct, iz)
    return pl.pallas_call(
        hand_out,
        out_shape=(jax.ShapeDtypeStruct(tile, f32), jax.ShapeDtypeStruct(tile, f32)),
        in_specs=[anywhere] * 2,
        out_specs=(hbm, hbm),
        scratch_shapes=[pltpu.SemaphoreType.DMA((2, 2))],
        compiler_params=pltpu.CompilerParams(vmem_limit_bytes=1024 * 1024),
    )(*results)


def solution(mesh):
    tile = P("gx", "gy", None)
    placed = (tile,) * 6 + (P("gx"), P("gx", None), P("gy"), P("gy", None), P(), P())
    return jax.shard_map(
        functools.partial(per_device, mesh.shape["gx"], mesh.shape["gy"]),
        mesh=mesh,
        in_specs=placed,
        out_specs=(tile, tile),
        check_vma=False,
    )
```

```python
import functools

import jax
import jax.numpy as jnp
from jax import lax
from jax.experimental import pallas as pl
from jax.experimental.pallas import tpu as pltpu
from jax.sharding import PartitionSpec as P

explicit_part = 2.0
heat_release = 100.0
cure_step = 0.5
arrhenius = 0.5
initial_rate = 0.1
MESH = pl.DeviceIdType.MESH
MARGIN = 8


def reduced_coefficients(ends, coef, count):
    corner = None
    for k in range(count - 1):
        upper = ends[k, 3:4]
        if corner is not None:
            upper = upper + ends[k, 1:2] * ends[k, 2:3] * corner
        head = ends[k + 1, 0:1]
        bottom = 1.0 / (1.0 - upper * head)
        corner = upper * bottom
        right_next = ends[k + 1, 2:3]
        coef[k, 0:1] = bottom
        coef[k, 1:2] = corner
        coef[k, 2:3] = head * bottom
        coef[k, 3:4] = ends[k, 1:2]
        coef[k, 4:5] = bottom * right_next
        coef[k, 5:6] = corner * right_next


def reduced_solve(first, last, coef, count):
    tops, lows = [], []
    for k in range(count - 1):
        shifted = last(k)
        if k:
            shifted = shifted + coef[k, 3:4] * tops[-1]
        follow = first(k + 1)
        tops.append(coef[k, 0:1] * shifted + coef[k, 1:2] * follow)
        lows.append(coef[k, 2:3] * shifted + coef[k, 0:1] * follow)
    for k in range(count - 3, -1, -1):
        tops[k] = tops[k] + coef[k, 5:6] * lows[k + 1]
        lows[k] = lows[k] + coef[k, 4:5] * lows[k + 1]
    zero = jnp.zeros_like(first(0))
    return lows + [zero], [zero] + tops


def kernel(
    nx,
    ny,
    ts_hbm,
    cs_hbm,
    tm_hbm,
    cm_hbm,
    al_hbm,
    ac_hbm,
    cf_hbm,
    bx_hbm,
    c2_hbm,
    by_hbm,
    ct_hbm,
    iz_hbm,
    out_t,
    out_c,
    cf,
    bxs,
    bx,
    c2,
    by,
    ct,
    iz,
    lu,
    lc,
    t_mid,
    c_mid,
    t_start,
    c_start,
    lu_second,
    lc_second,
    rate_t,
    rate_c,
    g,
    h,
    x_next,
    x_prev,
    mu,
    u,
    bycat,
    bxcat,
    izcat,
    diagonal,
    thick,
    cya,
    cyb,
    wy0,
    wy1,
    ly,
    ry,
    tm_coef,
    tc_coef,
    zr,
    exs,
    exr,
    eys,
    eyr,
    coefx,
    coefy,
    xas,
    xar,
    xbs,
    xbr,
    yas,
    yar,
    ybs,
    ybr,
    eas,
    ear,
    eay,
    ebs,
    ebr,
    ebx,
    load_sem,
    store_sem,
    gx_send,
    gx_recv,
    gy_send,
    gy_recv,
):
    lx, lyn, nz = lu.shape
    rx = lyn // nx
    ryn = lx // ny
    mex = lax.axis_index("gx")
    mey = lax.axis_index("gy")
    sides = {"gx": (nx, mex, gx_send, gx_recv), "gy": (ny, mey, gy_send, gy_recv)}

    barrier = pltpu.get_barrier_semaphore()
    for axis, (count, me, _, _) in sides.items():
        for k in range(1, count):
            pl.semaphore_signal(
                barrier,
                inc=1,
                device_id={axis: lax.rem(me + k, count)},
                device_id_type=MESH,
            )

    loads = [
        pltpu.make_async_copy(source, target, load_sem.at[n])
        for n, (source, target) in enumerate(
            (
                (cf_hbm, cf),
                (bx_hbm, bxs),
                (by_hbm, by),
                (bx_hbm, bx),
                (c2_hbm, c2),
                (al_hbm, lu),
                (iz_hbm, iz),
                (ct_hbm, ct),
                (tm_hbm, t_mid),
                (cm_hbm, c_mid),
                (ac_hbm, lc),
                (ts_hbm, t_start),
                (cs_hbm, c_start),
            )
        )
    ]
    for load in loads:
        load.start()

    started = []

    def exchange(axis, kind, source, target):
        count, me, send, recv = sides[axis]
        copies = []
        for k in range(1, count):
            peer = lax.rem(me + k, count)
            copy = pltpu.make_async_remote_copy(
                src_ref=source(peer),
                dst_ref=target,
                send_sem=send.at[kind, k],
                recv_sem=recv.at[kind, k],
                device_id={axis: peer},
                device_id_type=MESH,
            )
            copy.start()
            copies.append(copy)
        started.extend(copies)
        return copies

    def arrive(copies):
        for copy in copies:
            copy.wait_recv()

    def row(value):
        return jnp.broadcast_to(value, (1, nz))

    wide = 4
    chunk = 32
    bf16 = jnp.bfloat16

    def stack(matrix, target):
        size = matrix.shape[0]
        part0 = matrix.astype(bf16)
        rest = matrix - part0.astype(jnp.float32)
        part1 = rest.astype(bf16)
        part2 = (rest - part1.astype(jnp.float32)).astype(bf16)
        for n, part in enumerate((part0, part1, part2)):
            target[n * size : (n + 1) * size] = jnp.concatenate([part, part], axis=1)

    def parted(value):
        high = value.astype(bf16)
        return high, (value - high.astype(jnp.float32)).astype(bf16)

    def stacked_dot(parts, value):
        size = value.shape[0]
        done = jnp.dot(
            parts[...],
            jnp.concatenate(parted(value), axis=0),
            preferred_element_type=jnp.float32,
        )
        return (done[2 * size :] + done[size : 2 * size]) + done[0:size]

    def prepare():
        face_low = explicit_part * ct[0:nz].reshape(1, nz)
        face_high = explicit_part * ct[1 : nz + 1].reshape(1, nz)
        lane = lax.broadcasted_iota(jnp.int32, (1, nz), 1)
        thick[0:1] = jnp.where(lane == 0, 0.0, face_low)
        thick[1:2] = jnp.where(lane == nz - 1, 0.0, face_high)
        def second_faces(j, carry):
            low, high = explicit_part * c2[j], explicit_part * c2[j + 1]
            cya[pl.ds(j, 1)] = row(low)
            cyb[pl.ds(j, 1)] = row(high)
            diagonal[pl.ds(j, 1)] = face_low + face_high + (low + high)
            return carry

        lax.fori_loop(0, lyn, second_faces, 0, unroll=8)
        ly[...] = wy0[...] * s0
        ry[...] = wy1[...] * s1

        matrix = iz[...]
        part0 = matrix.astype(bf16)
        izcat[0] = part0
        izcat[1] = (matrix - part0.astype(jnp.float32)).astype(bf16)

    for n in range(5):
        loads[n].wait()
    stack(by[...], bycat)
    stack(bx[...], bxcat)
    wy0[...] = jnp.broadcast_to(by[:, 0:1], (lyn, nz))
    wy1[...] = jnp.broadcast_to(by[:, lyn - 1 : lyn], (lyn, nz))
    eas[...] = jnp.zeros_like(eas)
    ebs[...] = jnp.zeros_like(ebs)
    zr[...] = jnp.zeros_like(zr)
    exs[...] = jnp.zeros_like(exs)
    eys[...] = jnp.zeros_like(eys)
    empty = jnp.zeros((lyn, nz), jnp.float32)

    def fold(value):
        return jnp.sum(value.reshape(-1, 8, nz), axis=0)

    def eliminate(i, keep):
        partial = 1.0 + cf[i] * keep
        scale = 1.0 / (partial + cf[i + 1])
        tm_coef[i] = scale
        tc_coef[i] = cf[i + 1] * scale
        return partial * scale

    lax.fori_loop(0, lx, eliminate, jnp.ones((1, nz), jnp.float32), unroll=4)
    loads[5].wait()

    def tips(i, carry):
        first, last = carry
        slab = lu[i]
        u[0, 0, i] = fold(slab * wy0[...])
        u[1, 0, i] = fold(slab * wy1[...])
        return first + bxs[i, 0] * slab, last + bxs[i, lx - 1] * slab

    first, last = lax.fori_loop(0, lx, tips, (empty, empty), unroll=4)

    for step in range(2):
        temper, cure = ((t_mid, c_mid), (t_start, c_start))[step]
        lu_now, lc_now = ((lu, lc), (lu_second, lc_second))[step]
        lu_then, lc_then = ((lu_second, lc_second), (lu, lc))[step]
        tip_x = stacked_dot(bycat, jnp.concatenate([first, last], axis=1))
        for d in range(nx):
            xas[step, d, 0] = tip_x[d * rx : (d + 1) * rx, 0:nz]
            xas[step, d, 1] = tip_x[d * rx : (d + 1) * rx, nz:]
        if step == 0:
            a0, a1 = cf[0], cf[lx]
            exs[0:1] = row(a0 * bxs[0, 0])
            exs[1:2] = row(a0 * bxs[0, lx - 1])
            exs[2:3] = row(a1 * bxs[lx - 1, 0])
            exs[3:4] = row(a1 * bxs[lx - 1, lx - 1])
            s0, s1 = c2[0], c2[lyn]
            eys[0:1] = row(by[0:1, 0:1]) * s0
            eys[1:2] = row(by[0:1, lyn - 1 : lyn]) * s0
            eys[2:3] = row(by[lyn - 1 : lyn, 0:1]) * s1
            eys[3:4] = row(by[lyn - 1 : lyn, lyn - 1 : lyn]) * s1
            pl.semaphore_wait(barrier, nx + ny - 2)
        out_xa = exchange("gx", 1 + 3 * step, lambda peer: xas.at[step, peer], xar.at[step, mex])
        eas[step, 0:1] = tip_x[0:1, 0:nz]
        eas[step, 1:2] = tip_x[0:1, nz:]
        eas[step, 2:3] = tip_x[lyn - 1 : lyn, 0:nz]
        eas[step, 3:4] = tip_x[lyn - 1 : lyn, nz:]
        out_ea = exchange("gy", 3 + 3 * step, lambda peer: eas.at[step], ear.at[step, mey])
        folded = [u[n, 0] if step == 0 else u[n, 0] + u[n, 1] for n in range(2)]
        tip_y = stacked_dot(bxcat, jnp.concatenate([jnp.sum(f, axis=1) for f in folded], axis=1))
        for d in range(ny):
            yas[step, d, 0] = tip_y[d * ryn : (d + 1) * ryn, 0:nz]
            yas[step, d, 1] = tip_y[d * ryn : (d + 1) * ryn, nz:]
        out_ya = exchange("gy", 1 + 3 * step, lambda peer: yas.at[step, peer], yar.at[step, mey])
        xar[step, mex] = xas[step, mex]
        yar[step, mey] = yas[step, mey]
        ear[step, mey] = eas[step]

        if step == 0:
            ends_x = exchange("gx", 0, lambda peer: exs, exr.at[mex])
            ends_y = exchange("gy", 0, lambda peer: eys, eyr.at[mey])
            exr[mex] = exs[...]
            eyr[mey] = eys[...]
            loads[6].wait()
            loads[7].wait()
            prepare()

        def through(n, carry):
            block = lu_now[pl.ds(n * wide, wide)].reshape(wide * lyn, nz)
            high, low = parted(block)
            done = (
                jnp.dot(high, izcat[1], preferred_element_type=jnp.float32)
                + jnp.dot(low, izcat[0], preferred_element_type=jnp.float32)
                + jnp.dot(high, izcat[0], preferred_element_type=jnp.float32)
            )
            g[pl.ds(n * wide, wide)] = done.reshape(wide, lyn, nz)
            return carry

        lax.fori_loop(0, lx // wide, through, 0, unroll=2)

        def forward(n, before):
            solved = [stacked_dot(bycat, g[n * wide + k]) for k in range(wide)]
            for k in range(wide):
                i = n * wide + k
                before = (solved[k] + cf[i] * before) * tm_coef[i]
                h[i] = before
            return before

        if step == 1:
            lax.fori_loop(0, lx // wide, forward, empty)

        if step == 0:
            arrive(ends_x)
            arrive(ends_y)
            reduced_coefficients(exr, coefx, nx)
            reduced_coefficients(eyr, coefy, ny)
        arrive(out_xa)
        lows, tops = reduced_solve(
            lambda k: xar[step, k, 0], lambda k: xar[step, k, 1], coefx, nx
        )
        for d in range(nx):
            xbs[step, d, 0] = lows[d]
            xbs[step, d, 1] = tops[d]
        out_xb = exchange("gx", 2 + 3 * step, lambda peer: xbs.at[step, peer], xbr.at[step, mex])
        arrive(out_ea)
        lows, tops = reduced_solve(
            lambda k: ear[step, k, 0:2], lambda k: ear[step, k, 2:4], coefy, ny
        )
        for d in range(ny):
            eay[d, 0:2] = lows[d]
            eay[d, 2:4] = tops[d]
        edge = eay[mey]
        ebs[step, 0:1] = edge[0:1]
        ebs[step, 1:2] = edge[2:3]
        ebs[step, 2:3] = edge[1:2]
        ebs[step, 3:4] = edge[3:4]
        out_eb = exchange("gx", 3 + 3 * step, lambda peer: ebs.at[step], ebr.at[step, mex])
        arrive(out_ya)
        lows, tops = reduced_solve(
            lambda k: yar[step, k, 0], lambda k: yar[step, k, 1], coefy, ny
        )
        for d in range(ny):
            ybs[step, d, 0] = lows[d]
            ybs[step, d, 1] = tops[d]
        out_yb = exchange("gy", 2 + 3 * step, lambda peer: ybs.at[step, peer], ybr.at[step, mey])
        xbr[step, mex] = xbs[step, mex]
        ybr[step, mey] = ybs[step, mey]
        ebr[step, mex] = ebs[step]

        inside = slice(MARGIN, MARGIN + lyn)

        if step == 0:
            lax.fori_loop(0, lx // wide, forward, empty)

        def backward(n, after):
            i = lx - 1 - n
            value = h[i] + tc_coef[i] * after
            g[i] = value
            return value

        lax.fori_loop(0, lx, backward, empty, unroll=4)

        if step == 0:
            for n in (8, 9, 10):
                loads[n].wait()
        else:
            loads[11].wait()
            loads[12].wait()

        def rates(i, carry):
            heating = jnp.exp(arrhenius * temper[i])
            value = cure[i]
            remain = 1.0 - value
            grown = initial_rate + value
            rate_t[i] = (heat_release * arrhenius) * (heating * grown * remain * remain)
            rate_c[i] = (heat_release * heating) * (remain * remain - 2.0 * grown * remain)
            return carry

        lax.fori_loop(0, lx, rates, 0, unroll=2)

        arrive(out_eb)
        lows, tops = reduced_solve(
            lambda k: ebr[step, k, 0:2], lambda k: ebr[step, k, 2:4], coefx, nx
        )
        for d in range(nx):
            ebx[d, 0:2] = lows[d]
            ebx[d, 2:4] = tops[d]
        arrive(out_xb)
        arrive(out_yb)
        for d in range(nx):
            zr[d * rx : (d + 1) * rx] = xbr[step, d, 0]
            zr[lyn + d * rx : lyn + (d + 1) * rx] = xbr[step, d, 1]
        base = 2 * lyn
        for d in range(ny):
            zr[base + d * ryn : base + (d + 1) * ryn] = ybr[step, d, 0]
            zr[base + lx + d * ryn : base + lx + (d + 1) * ryn] = ybr[step, d, 1]
        corner = base + 2 * lx
        zr[corner : corner + 4] = ebx[mex, 0:4]
        ends = zr[...]
        high, low = parted(ends)
        rest = ((ends - high.astype(jnp.float32)) - low.astype(jnp.float32)).astype(bf16)
        count = ends.shape[0]
        main = jnp.dot(
            jnp.concatenate([high, low, rest], axis=0), izcat[0], preferred_element_type=jnp.float32
        )
        fine = jnp.dot(
            jnp.concatenate([high, low], axis=0), izcat[1], preferred_element_type=jnp.float32
        )
        zr[...] = (
            (main[2 * count :] + fine[count:]) + (main[count : 2 * count] + fine[0:count])
        ) + main[0:count]
        next_next = zr[corner : corner + 1]
        next_prev = zr[corner + 1 : corner + 2]
        prev_next = zr[corner + 2 : corner + 3]
        prev_prev = zr[corner + 3 : corner + 4]
        value = zr[0:lyn] + ly[...] * next_prev + ry[...] * next_next
        x_next[...] = value
        mu[lx + 1, inside] = value
        value = zr[lyn : 2 * lyn] + ly[...] * prev_prev + ry[...] * prev_next
        x_prev[...] = value
        mu[0, inside] = value

        def correct(i, carry):
            left = a0 * bxs[0, i]
            right = a1 * bxs[lx - 1, i]
            y_next = zr[pl.ds(base + i, 1)]
            y_prev = zr[pl.ds(base + lx + i, 1)]
            mu[i + 1, inside] = (
                g[i]
                + left * x_prev[...]
                + right * x_next[...]
                + ly[...] * y_prev
                + ry[...] * y_next
            )
            mu[i + 1, MARGIN - 1 : MARGIN] = y_prev + left * prev_prev + right * next_prev
            mu[i + 1, MARGIN + lyn : MARGIN + lyn + 1] = (
                y_next + left * prev_next + right * next_next
            )
            return carry

        lax.fori_loop(0, lx, correct, 0, unroll=4)

        stores = []
        firsts, lasts = [], []
        group = 4
        for part, y in enumerate(range(0, lyn, chunk)):
            here = slice(y, y + chunk)
            start = MARGIN + y

            def update(n, carry):
                first, last = carry
                i = n * group
                flux = (explicit_part * cf[i]) * (
                    mu[i + 1, start : start + chunk] - mu[i, start : start + chunk]
                )
                for k in range(group):
                    i = n * group + k
                    value = mu[i + 1, start : start + chunk]
                    follow = (explicit_part * cf[i + 1]) * (
                        mu[i + 2, start : start + chunk] - value
                    )
                    kick = (
                        (flux - follow)
                        + diagonal[here] * value
                        - cya[here] * mu[i + 1, start - 1 : start + chunk - 1]
                        - cyb[here] * mu[i + 1, start + 1 : start + chunk + 1]
                        - thick[0:1] * pltpu.roll(value, 1, 1)
                        - thick[1:2] * pltpu.roll(value, nz - 1, 1)
                    )
                    flux = follow
                    old = lc_now[i, here]
                    source = value + (cure_step / heat_release) * old
                    new = lu_now[i, here] - kick + rate_t[i, here] * source
                    lu_then[i, here] = new
                    lc_then[i, here] = old + rate_c[i, here] * source
                    if step == 0:
                        first = first + bxs[i, 0] * new
                        last = last + bxs[i, lx - 1] * new
                        u[0, part, i] = fold(new * wy0[here])
                        u[1, part, i] = fold(new * wy1[here])
                return first, last

            none = jnp.zeros((chunk, nz), jnp.float32)
            first, last = lax.fori_loop(0, lx // group, update, (none, none))
            firsts.append(first)
            lasts.append(last)
            if step == 1:
                for n, (source, target) in enumerate(((lu, out_t), (lc, out_c))):
                    store = pltpu.make_async_copy(
                        source.at[:, pl.ds(y, chunk)],
                        target.at[:, pl.ds(y, chunk)],
                        store_sem.at[n, part],
                    )
                    store.start()
                    stores.append(store)
        first = jnp.concatenate(firsts, axis=0)
        last = jnp.concatenate(lasts, axis=0)
        for store in stores:
            store.wait()
    for copy in started:
        copy.wait_send()


def hand_out(first, second, out_first, out_second, sem):
    half = first.shape[0] // 4
    copies = [
        pltpu.make_async_copy(
            source.at[pl.ds(part * half, half)], target.at[pl.ds(part * half, half)], sem.at[n, part]
        )
        for n, (source, target) in enumerate(((first, out_first), (second, out_second)))
        for part in range(4)
    ]
    for copy in copies:
        copy.start()
    for copy in copies:
        copy.wait()


def per_device(nx, ny, ts, cs, tm, cm, al, ac, cf, bx, c2, by, ct, iz):
    lx, lyn, nz = al.shape
    f32 = jnp.float32
    vm = pltpu.VMEM
    tile = (lx, lyn, nz)
    anywhere = pl.BlockSpec(memory_space=pl.ANY)
    hbm = pl.BlockSpec(memory_space=pltpu.HBM)
    sm = pltpu.SMEM
    rx, ryn = lyn // nx, lx // ny
    scratch = (
        [sm(cf.shape, f32), sm(bx.shape, f32), vm(bx.shape, f32), sm(c2.shape, f32)]
        + [vm(by.shape, f32), vm((nz + 1,), f32), vm(iz.shape, f32)]
        + [vm(tile, f32)] * 12
        + [vm((lyn, nz), f32)] * 2
        + [vm((lx + 2, lyn + 2 * MARGIN, nz), f32), vm((2, 2, lx, 8, nz), f32)]
        + [vm((3 * lyn, 2 * lyn), jnp.bfloat16), vm((3 * lx, 2 * lx), jnp.bfloat16)]
        + [vm((2, nz, nz), jnp.bfloat16), vm((lyn, nz), f32), vm((8, nz), f32)]
        + [vm((lyn, nz), f32)] * 6
        + [vm((lx, 1, nz), f32)] * 2
        + [vm((2 * lyn + 2 * lx + 16, nz), f32)]
        + [vm((8, nz), f32), vm((nx, 8, nz), f32), vm((8, nz), f32), vm((ny, 8, nz), f32)]
        + [vm((nx, 8, nz), f32), vm((ny, 8, nz), f32)]
        + [vm((2, nx, 2, rx, nz), f32)] * 4
        + [vm((2, ny, 2, ryn, nz), f32)] * 4
        + [vm((2, 8, nz), f32), vm((2, ny, 8, nz), f32), vm((ny, 8, nz), f32)]
        + [vm((2, 8, nz), f32), vm((2, nx, 8, nz), f32), vm((nx, 8, nz), f32)]
        + [pltpu.SemaphoreType.DMA((13,)), pltpu.SemaphoreType.DMA((2, lyn // 32))]
        + [pltpu.SemaphoreType.DMA((7, nx))] * 2
        + [pltpu.SemaphoreType.DMA((7, ny))] * 2
    )
    results = pl.pallas_call(
        functools.partial(kernel, nx, ny),
        out_shape=(jax.ShapeDtypeStruct(tile, f32), jax.ShapeDtypeStruct(tile, f32)),
        in_specs=[hbm] * 12,
        out_specs=(anywhere, anywhere),
        scratch_shapes=scratch,
        compiler_params=pltpu.CompilerParams(
            collective_id=0, has_side_effects=True, vmem_limit_bytes=60 * 1024 * 1024
        ),
    )(ts, cs, tm, cm, al, ac, cf, bx, c2, by, ct, iz)
    return pl.pallas_call(
        hand_out,
        out_shape=(jax.ShapeDtypeStruct(tile, f32), jax.ShapeDtypeStruct(tile, f32)),
        in_specs=[anywhere] * 2,
        out_specs=(hbm, hbm),
        scratch_shapes=[pltpu.SemaphoreType.DMA((2, 4))],
        compiler_params=pltpu.CompilerParams(vmem_limit_bytes=60 * 1024 * 1024),
    )(*results)


def solution(mesh):
    tile = P("gx", "gy", None)
    placed = (tile,) * 6 + (P("gx"), P("gx", None), P("gy"), P("gy", None), P(), P())
    return jax.shard_map(
        functools.partial(per_device, mesh.shape["gx"], mesh.shape["gy"]),
        mesh=mesh,
        in_specs=placed,
        out_specs=(tile, tile),
        check_vma=False,
    )
```

```python
import functools

import jax
import jax.numpy as jnp
from jax import lax
from jax.experimental import pallas as pl
from jax.experimental.pallas import tpu as pltpu
from jax.sharding import PartitionSpec as P

explicit_part = 2.0
heat_release = 100.0
cure_step = 0.5
arrhenius = 0.5
initial_rate = 0.1
MESH = pl.DeviceIdType.MESH
MARGIN = 8


def reduced_coefficients(ends, coef, count):
    corner = None
    for k in range(count - 1):
        upper = ends[k, 3:4]
        if corner is not None:
            upper = upper + ends[k, 1:2] * ends[k, 2:3] * corner
        head = ends[k + 1, 0:1]
        bottom = 1.0 / (1.0 - upper * head)
        corner = upper * bottom
        right_next = ends[k + 1, 2:3]
        coef[k, 0:1] = bottom
        coef[k, 1:2] = corner
        coef[k, 2:3] = head * bottom
        coef[k, 3:4] = ends[k, 1:2]
        coef[k, 4:5] = bottom * right_next
        coef[k, 5:6] = corner * right_next


def reduced_solve(first, last, coef, count):
    tops, lows = [], []
    for k in range(count - 1):
        shifted = last(k)
        if k:
            shifted = shifted + coef[k, 3:4] * tops[-1]
        follow = first(k + 1)
        tops.append(coef[k, 0:1] * shifted + coef[k, 1:2] * follow)
        lows.append(coef[k, 2:3] * shifted + coef[k, 0:1] * follow)
    for k in range(count - 3, -1, -1):
        tops[k] = tops[k] + coef[k, 5:6] * lows[k + 1]
        lows[k] = lows[k] + coef[k, 4:5] * lows[k + 1]
    zero = jnp.zeros_like(first(0))
    return lows + [zero], [zero] + tops


def kernel(
    nx,
    ny,
    ts_hbm,
    cs_hbm,
    tm_hbm,
    cm_hbm,
    al_hbm,
    ac_hbm,
    cf_hbm,
    bx_hbm,
    c2_hbm,
    by_hbm,
    ct_hbm,
    iz_hbm,
    out_t,
    out_c,
    cf,
    bxs,
    bx,
    c2,
    by,
    ct,
    iz,
    lu,
    lc,
    t_mid,
    c_mid,
    t_start,
    c_start,
    lu_second,
    lc_second,
    rate_t,
    rate_c,
    g,
    h,
    x_next,
    x_prev,
    mu,
    u,
    bycat,
    bxcat,
    izcat,
    diagonal,
    thick,
    cya,
    cyb,
    wy0,
    wy1,
    ly,
    ry,
    tm_coef,
    tc_coef,
    zr,
    exs,
    exr,
    eys,
    eyr,
    coefx,
    coefy,
    xas,
    xar,
    xbs,
    xbr,
    yas,
    yar,
    ybs,
    ybr,
    eas,
    ear,
    eay,
    ebs,
    ebr,
    ebx,
    load_sem,
    store_sem,
    gx_send,
    gx_recv,
    gy_send,
    gy_recv,
):
    lx, lyn, nz = lu.shape
    rx = lyn // nx
    ryn = lx // ny
    mex = lax.axis_index("gx")
    mey = lax.axis_index("gy")
    sides = {"gx": (nx, mex, gx_send, gx_recv), "gy": (ny, mey, gy_send, gy_recv)}

    barrier = pltpu.get_barrier_semaphore()
    for axis, (count, me, _, _) in sides.items():
        for k in range(1, count):
            pl.semaphore_signal(
                barrier,
                inc=1,
                device_id={axis: lax.rem(me + k, count)},
                device_id_type=MESH,
            )

    quarter = lx // 4
    loads = [
        pltpu.make_async_copy(source, target, load_sem.at[n])
        for n, (source, target) in enumerate(
            (
                (cf_hbm, cf),
                (bx_hbm, bxs),
                (by_hbm, by),
                (bx_hbm, bx),
                (c2_hbm, c2),
                *(
                    (al_hbm.at[pl.ds(k * quarter, quarter)], lu.at[pl.ds(k * quarter, quarter)])
                    for k in range(4)
                ),
                (iz_hbm, iz),
                (ct_hbm, ct),
                (tm_hbm, t_mid),
                (cm_hbm, c_mid),
                (ac_hbm, lc),
                (ts_hbm, t_start),
                (cs_hbm, c_start),
            )
        )
    ]
    for load in loads:
        load.start()

    started = []

    def exchange(axis, kind, source, target):
        count, me, send, recv = sides[axis]
        copies = []
        for k in range(1, count):
            peer = lax.rem(me + k, count)
            copy = pltpu.make_async_remote_copy(
                src_ref=source(peer),
                dst_ref=target,
                send_sem=send.at[kind, k],
                recv_sem=recv.at[kind, k],
                device_id={axis: peer},
                device_id_type=MESH,
            )
            copy.start()
            copies.append(copy)
        started.extend(copies)
        return copies

    def arrive(copies):
        for copy in copies:
            copy.wait_recv()

    def row(value):
        return jnp.broadcast_to(value, (1, nz))

    wide = 4
    many = 8
    chunk = 32
    bf16 = jnp.bfloat16

    def stack(matrix, target):
        size = matrix.shape[0]
        part0 = matrix.astype(bf16)
        rest = matrix - part0.astype(jnp.float32)
        part1 = rest.astype(bf16)
        part2 = (rest - part1.astype(jnp.float32)).astype(bf16)
        for n, part in enumerate((part0, part1, part2)):
            target[n * size : (n + 1) * size] = jnp.concatenate([part, part], axis=1)

    def parted(value):
        high = value.astype(bf16)
        return high, (value - high.astype(jnp.float32)).astype(bf16)

    def stacked_dot(parts, value):
        size = value.shape[0]
        done = jnp.dot(
            parts[...],
            jnp.concatenate(parted(value), axis=0),
            preferred_element_type=jnp.float32,
        )
        return (done[2 * size :] + done[size : 2 * size]) + done[0:size]

    def prepare():
        face_low = explicit_part * ct[0:nz].reshape(1, nz)
        face_high = explicit_part * ct[1 : nz + 1].reshape(1, nz)
        lane = lax.broadcasted_iota(jnp.int32, (1, nz), 1)
        thick[0:1] = jnp.where(lane == 0, 0.0, face_low)
        thick[1:2] = jnp.where(lane == nz - 1, 0.0, face_high)
        def second_faces(j, carry):
            low, high = explicit_part * c2[j], explicit_part * c2[j + 1]
            cya[pl.ds(j, 1)] = row(low)
            cyb[pl.ds(j, 1)] = row(high)
            diagonal[pl.ds(j, 1)] = face_low + face_high + (low + high)
            return carry

        lax.fori_loop(0, lyn, second_faces, 0, unroll=8)
        ly[...] = wy0[...] * s0
        ry[...] = wy1[...] * s1

        matrix = iz[...]
        part0 = matrix.astype(bf16)
        izcat[0] = part0
        izcat[1] = (matrix - part0.astype(jnp.float32)).astype(bf16)

    for n in range(5):
        loads[n].wait()
    stack(by[...], bycat)
    stack(bx[...], bxcat)
    wy0[...] = jnp.broadcast_to(by[:, 0:1], (lyn, nz))
    wy1[...] = jnp.broadcast_to(by[:, lyn - 1 : lyn], (lyn, nz))
    eas[...] = jnp.zeros_like(eas)
    ebs[...] = jnp.zeros_like(ebs)
    zr[...] = jnp.zeros_like(zr)
    exs[...] = jnp.zeros_like(exs)
    eys[...] = jnp.zeros_like(eys)
    empty = jnp.zeros((lyn, nz), jnp.float32)

    def fold(value):
        return jnp.sum(value.reshape(-1, 8, nz), axis=0)

    def eliminate(i, keep):
        partial = 1.0 + cf[i] * keep
        scale = 1.0 / (partial + cf[i + 1])
        tm_coef[i] = scale
        tc_coef[i] = cf[i + 1] * scale
        return partial * scale

    lax.fori_loop(0, lx, eliminate, jnp.ones((1, nz), jnp.float32), unroll=4)
    def tips(i, carry):
        first, last = carry
        slab = lu[i]
        u[0, 0, i] = fold(slab * wy0[...])
        u[1, 0, i] = fold(slab * wy1[...])
        return first + bxs[i, 0] * slab, last + bxs[i, lx - 1] * slab

    first = last = empty
    for k in range(4):
        loads[5 + k].wait()
        first, last = lax.fori_loop(
            k * quarter, (k + 1) * quarter, tips, (first, last), unroll=4
        )

    for step in range(2):
        temper, cure = ((t_mid, c_mid), (t_start, c_start))[step]
        lu_now, lc_now = ((lu, lc), (lu_second, lc_second))[step]
        lu_then, lc_then = ((lu_second, lc_second), (lu, lc))[step]
        tip_x = stacked_dot(bycat, jnp.concatenate([first, last], axis=1))
        for d in range(nx):
            xas[step, d, 0] = tip_x[d * rx : (d + 1) * rx, 0:nz]
            xas[step, d, 1] = tip_x[d * rx : (d + 1) * rx, nz:]
        if step == 0:
            a0, a1 = cf[0], cf[lx]
            exs[0:1] = row(a0 * bxs[0, 0])
            exs[1:2] = row(a0 * bxs[0, lx - 1])
            exs[2:3] = row(a1 * bxs[lx - 1, 0])
            exs[3:4] = row(a1 * bxs[lx - 1, lx - 1])
            s0, s1 = c2[0], c2[lyn]
            eys[0:1] = row(by[0:1, 0:1]) * s0
            eys[1:2] = row(by[0:1, lyn - 1 : lyn]) * s0
            eys[2:3] = row(by[lyn - 1 : lyn, 0:1]) * s1
            eys[3:4] = row(by[lyn - 1 : lyn, lyn - 1 : lyn]) * s1
            pl.semaphore_wait(barrier, nx + ny - 2)
        out_xa = exchange("gx", 1 + 3 * step, lambda peer: xas.at[step, peer], xar.at[step, mex])
        eas[step, 0:1] = tip_x[0:1, 0:nz]
        eas[step, 1:2] = tip_x[0:1, nz:]
        eas[step, 2:3] = tip_x[lyn - 1 : lyn, 0:nz]
        eas[step, 3:4] = tip_x[lyn - 1 : lyn, nz:]
        out_ea = exchange("gy", 3 + 3 * step, lambda peer: eas.at[step], ear.at[step, mey])
        folded = [u[n, 0] if step == 0 else u[n, 0] + u[n, 1] for n in range(2)]
        tip_y = stacked_dot(bxcat, jnp.concatenate([jnp.sum(f, axis=1) for f in folded], axis=1))
        for d in range(ny):
            yas[step, d, 0] = tip_y[d * ryn : (d + 1) * ryn, 0:nz]
            yas[step, d, 1] = tip_y[d * ryn : (d + 1) * ryn, nz:]
        out_ya = exchange("gy", 1 + 3 * step, lambda peer: yas.at[step, peer], yar.at[step, mey])
        xar[step, mex] = xas[step, mex]
        yar[step, mey] = yas[step, mey]
        ear[step, mey] = eas[step]

        if step == 0:
            ends_x = exchange("gx", 0, lambda peer: exs, exr.at[mex])
            ends_y = exchange("gy", 0, lambda peer: eys, eyr.at[mey])
            exr[mex] = exs[...]
            eyr[mey] = eys[...]
            loads[9].wait()
            loads[10].wait()
            prepare()

        def through(n, carry):
            block = lu_now[pl.ds(n * many, many)].reshape(many * lyn, nz)
            high, low = parted(block)
            done = (
                jnp.dot(high, izcat[1], preferred_element_type=jnp.float32)
                + jnp.dot(low, izcat[0], preferred_element_type=jnp.float32)
                + jnp.dot(high, izcat[0], preferred_element_type=jnp.float32)
            )
            g[pl.ds(n * many, many)] = done.reshape(many, lyn, nz)
            return carry

        lax.fori_loop(0, lx // many, through, 0)

        def forward(n, before):
            solved = [stacked_dot(bycat, g[n * wide + k]) for k in range(wide)]
            for k in range(wide):
                i = n * wide + k
                before = (solved[k] + cf[i] * before) * tm_coef[i]
                h[i] = before
            return before

        if step == 1:
            lax.fori_loop(0, lx // wide, forward, empty)

        if step == 0:
            arrive(ends_x)
            arrive(ends_y)
            reduced_coefficients(exr, coefx, nx)
            reduced_coefficients(eyr, coefy, ny)
        arrive(out_xa)
        lows, tops = reduced_solve(
            lambda k: xar[step, k, 0], lambda k: xar[step, k, 1], coefx, nx
        )
        for d in range(nx):
            xbs[step, d, 0] = lows[d]
            xbs[step, d, 1] = tops[d]
        out_xb = exchange("gx", 2 + 3 * step, lambda peer: xbs.at[step, peer], xbr.at[step, mex])
        arrive(out_ea)
        lows, tops = reduced_solve(
            lambda k: ear[step, k, 0:2], lambda k: ear[step, k, 2:4], coefy, ny
        )
        for d in range(ny):
            eay[d, 0:2] = lows[d]
            eay[d, 2:4] = tops[d]
        edge = eay[mey]
        ebs[step, 0:1] = edge[0:1]
        ebs[step, 1:2] = edge[2:3]
        ebs[step, 2:3] = edge[1:2]
        ebs[step, 3:4] = edge[3:4]
        out_eb = exchange("gx", 3 + 3 * step, lambda peer: ebs.at[step], ebr.at[step, mex])
        arrive(out_ya)
        lows, tops = reduced_solve(
            lambda k: yar[step, k, 0], lambda k: yar[step, k, 1], coefy, ny
        )
        for d in range(ny):
            ybs[step, d, 0] = lows[d]
            ybs[step, d, 1] = tops[d]
        out_yb = exchange("gy", 2 + 3 * step, lambda peer: ybs.at[step, peer], ybr.at[step, mey])
        xbr[step, mex] = xbs[step, mex]
        ybr[step, mey] = ybs[step, mey]
        ebr[step, mex] = ebs[step]

        inside = slice(MARGIN, MARGIN + lyn)

        if step == 0:
            lax.fori_loop(0, lx // wide, forward, empty)

        def backward(n, after):
            i = lx - 1 - n
            value = h[i] + tc_coef[i] * after
            g[i] = value
            return value

        lax.fori_loop(0, lx, backward, empty, unroll=4)

        if step == 0:
            for n in (11, 12, 13):
                loads[n].wait()
        else:
            loads[14].wait()
            loads[15].wait()

        def rates(i, carry):
            heating = jnp.exp(arrhenius * temper[i])
            value = cure[i]
            remain = 1.0 - value
            grown = initial_rate + value
            rate_t[i] = (heat_release * arrhenius) * (heating * grown * remain * remain)
            rate_c[i] = (heat_release * heating) * (remain * remain - 2.0 * grown * remain)
            return carry

        lax.fori_loop(0, lx, rates, 0, unroll=2)

        arrive(out_eb)
        lows, tops = reduced_solve(
            lambda k: ebr[step, k, 0:2], lambda k: ebr[step, k, 2:4], coefx, nx
        )
        for d in range(nx):
            ebx[d, 0:2] = lows[d]
            ebx[d, 2:4] = tops[d]
        arrive(out_xb)
        arrive(out_yb)
        for d in range(nx):
            zr[d * rx : (d + 1) * rx] = xbr[step, d, 0]
            zr[lyn + d * rx : lyn + (d + 1) * rx] = xbr[step, d, 1]
        base = 2 * lyn
        for d in range(ny):
            zr[base + d * ryn : base + (d + 1) * ryn] = ybr[step, d, 0]
            zr[base + lx + d * ryn : base + lx + (d + 1) * ryn] = ybr[step, d, 1]
        corner = base + 2 * lx
        zr[corner : corner + 4] = ebx[mex, 0:4]
        ends = zr[...]
        high, low = parted(ends)
        rest = ((ends - high.astype(jnp.float32)) - low.astype(jnp.float32)).astype(bf16)
        count = ends.shape[0]
        main = jnp.dot(
            jnp.concatenate([high, low, rest], axis=0), izcat[0], preferred_element_type=jnp.float32
        )
        fine = jnp.dot(
            jnp.concatenate([high, low], axis=0), izcat[1], preferred_element_type=jnp.float32
        )
        zr[...] = (
            (main[2 * count :] + fine[count:]) + (main[count : 2 * count] + fine[0:count])
        ) + main[0:count]
        next_next = zr[corner : corner + 1]
        next_prev = zr[corner + 1 : corner + 2]
        prev_next = zr[corner + 2 : corner + 3]
        prev_prev = zr[corner + 3 : corner + 4]
        value = zr[0:lyn] + ly[...] * next_prev + ry[...] * next_next
        x_next[...] = value
        mu[lx + 1, inside] = value
        value = zr[lyn : 2 * lyn] + ly[...] * prev_prev + ry[...] * prev_next
        x_prev[...] = value
        mu[0, inside] = value

        def correct(i, carry):
            left = a0 * bxs[0, i]
            right = a1 * bxs[lx - 1, i]
            y_next = zr[pl.ds(base + i, 1)]
            y_prev = zr[pl.ds(base + lx + i, 1)]
            mu[i + 1, inside] = (
                g[i]
                + left * x_prev[...]
                + right * x_next[...]
                + ly[...] * y_prev
                + ry[...] * y_next
            )
            mu[i + 1, MARGIN - 1 : MARGIN] = y_prev + left * prev_prev + right * next_prev
            mu[i + 1, MARGIN + lyn : MARGIN + lyn + 1] = (
                y_next + left * prev_next + right * next_next
            )
            return carry

        lax.fori_loop(0, lx, correct, 0, unroll=4)

        stores = []
        firsts, lasts = [], []
        group = 4
        for part, y in enumerate(range(0, lyn, chunk)):
            here = slice(y, y + chunk)
            start = MARGIN + y

            def update(n, carry):
                first, last = carry
                i = n * group
                flux = (explicit_part * cf[i]) * (
                    mu[i + 1, start : start + chunk] - mu[i, start : start + chunk]
                )
                for k in range(group):
                    i = n * group + k
                    value = mu[i + 1, start : start + chunk]
                    follow = (explicit_part * cf[i + 1]) * (
                        mu[i + 2, start : start + chunk] - value
                    )
                    kick = (
                        (flux - follow)
                        + diagonal[here] * value
                        - cya[here] * mu[i + 1, start - 1 : start + chunk - 1]
                        - cyb[here] * mu[i + 1, start + 1 : start + chunk + 1]
                        - thick[0:1] * pltpu.roll(value, 1, 1)
                        - thick[1:2] * pltpu.roll(value, nz - 1, 1)
                    )
                    flux = follow
                    old = lc_now[i, here]
                    source = value + (cure_step / heat_release) * old
                    new = lu_now[i, here] - kick + rate_t[i, here] * source
                    lu_then[i, here] = new
                    lc_then[i, here] = old + rate_c[i, here] * source
                    if step == 0:
                        first = first + bxs[i, 0] * new
                        last = last + bxs[i, lx - 1] * new
                        u[0, part, i] = fold(new * wy0[here])
                        u[1, part, i] = fold(new * wy1[here])
                return first, last

            none = jnp.zeros((chunk, nz), jnp.float32)
            first = last = none
            steps = lx // group // 2
            for half in range(2):
                first, last = lax.fori_loop(
                    half * steps, (half + 1) * steps, update, (first, last)
                )
                if step == 1:
                    rows = pl.ds(half * steps * group, steps * group)
                    for n, (source, target) in enumerate(((lu, out_t), (lc, out_c))):
                        store = pltpu.make_async_copy(
                            source.at[rows, pl.ds(y, chunk)],
                            target.at[rows, pl.ds(y, chunk)],
                            store_sem.at[n, part, half],
                        )
                        store.start()
                        stores.append(store)
            firsts.append(first)
            lasts.append(last)
        first = jnp.concatenate(firsts, axis=0)
        last = jnp.concatenate(lasts, axis=0)
        for store in stores:
            store.wait()
    for copy in started:
        copy.wait_send()


def hand_out(first, second, out_first, out_second, held, sem):
    chunks = held.shape[1]
    size = first.shape[0] // chunks
    arrivals, departures = [], []
    for part in range(chunks):
        rows = pl.ds(part * size, size)
        for n, (source, target) in enumerate(((first, out_first), (second, out_second))):
            slot = held.at[n, part]
            arrivals.append(pltpu.make_async_copy(source.at[rows], slot, sem.at[0, n, part]))
            departures.append(pltpu.make_async_copy(slot, target.at[rows], sem.at[1, n, part]))
    for copy in arrivals:
        copy.start()
    for arrival, departure in zip(arrivals, departures):
        arrival.wait()
        departure.start()
    for copy in departures:
        copy.wait()


def per_device(nx, ny, ts, cs, tm, cm, al, ac, cf, bx, c2, by, ct, iz):
    lx, lyn, nz = al.shape
    f32 = jnp.float32
    vm = pltpu.VMEM
    tile = (lx, lyn, nz)
    anywhere = pl.BlockSpec(memory_space=pl.ANY)
    hbm = pl.BlockSpec(memory_space=pltpu.HBM)
    sm = pltpu.SMEM
    rx, ryn = lyn // nx, lx // ny
    scratch = (
        [sm(cf.shape, f32), sm(bx.shape, f32), vm(bx.shape, f32), sm(c2.shape, f32)]
        + [vm(by.shape, f32), vm((nz + 1,), f32), vm(iz.shape, f32)]
        + [vm(tile, f32)] * 12
        + [vm((lyn, nz), f32)] * 2
        + [vm((lx + 2, lyn + 2 * MARGIN, nz), f32), vm((2, 2, lx, 8, nz), f32)]
        + [vm((3 * lyn, 2 * lyn), jnp.bfloat16), vm((3 * lx, 2 * lx), jnp.bfloat16)]
        + [vm((2, nz, nz), jnp.bfloat16), vm((lyn, nz), f32), vm((8, nz), f32)]
        + [vm((lyn, nz), f32)] * 6
        + [vm((lx, 1, nz), f32)] * 2
        + [vm((2 * lyn + 2 * lx + 16, nz), f32)]
        + [vm((8, nz), f32), vm((nx, 8, nz), f32), vm((8, nz), f32), vm((ny, 8, nz), f32)]
        + [vm((nx, 8, nz), f32), vm((ny, 8, nz), f32)]
        + [vm((2, nx, 2, rx, nz), f32)] * 4
        + [vm((2, ny, 2, ryn, nz), f32)] * 4
        + [vm((2, 8, nz), f32), vm((2, ny, 8, nz), f32), vm((ny, 8, nz), f32)]
        + [vm((2, 8, nz), f32), vm((2, nx, 8, nz), f32), vm((nx, 8, nz), f32)]
        + [pltpu.SemaphoreType.DMA((16,)), pltpu.SemaphoreType.DMA((2, lyn // 32, 2))]
        + [pltpu.SemaphoreType.DMA((7, nx))] * 2
        + [pltpu.SemaphoreType.DMA((7, ny))] * 2
    )
    results = pl.pallas_call(
        functools.partial(kernel, nx, ny),
        out_shape=(jax.ShapeDtypeStruct(tile, f32), jax.ShapeDtypeStruct(tile, f32)),
        in_specs=[hbm] * 12,
        out_specs=(anywhere, anywhere),
        scratch_shapes=scratch,
        compiler_params=pltpu.CompilerParams(
            collective_id=0, has_side_effects=True, vmem_limit_bytes=60 * 1024 * 1024
        ),
    )(ts, cs, tm, cm, al, ac, cf, bx, c2, by, ct, iz)
    return pl.pallas_call(
        hand_out,
        out_shape=(jax.ShapeDtypeStruct(tile, f32), jax.ShapeDtypeStruct(tile, f32)),
        in_specs=[anywhere] * 2,
        out_specs=(hbm, hbm),
        scratch_shapes=[vm((2, 8, lx // 8, lyn, nz), f32), pltpu.SemaphoreType.DMA((2, 2, 8))],
        compiler_params=pltpu.CompilerParams(vmem_limit_bytes=60 * 1024 * 1024),
    )(*results)


def solution(mesh):
    tile = P("gx", "gy", None)
    placed = (tile,) * 6 + (P("gx"), P("gx", None), P("gy"), P("gy", None), P(), P())
    return jax.shard_map(
        functools.partial(per_device, mesh.shape["gx"], mesh.shape["gy"]),
        mesh=mesh,
        in_specs=placed,
        out_specs=(tile, tile),
        check_vma=False,
    )
```

```python
import functools

import jax
import jax.numpy as jnp
from jax import lax
from jax.experimental import pallas as pl
from jax.experimental.pallas import tpu as pltpu
from jax.sharding import PartitionSpec as P

explicit_part = 2.0
heat_release = 100.0
cure_step = 0.5
arrhenius = 0.5
initial_rate = 0.1
MESH = pl.DeviceIdType.MESH
MARGIN = 8


def reduced_coefficients(ends, coef, count):
    corner = None
    for k in range(count - 1):
        upper = ends[k, 3:4]
        if corner is not None:
            upper = upper + ends[k, 1:2] * ends[k, 2:3] * corner
        head = ends[k + 1, 0:1]
        bottom = 1.0 / (1.0 - upper * head)
        corner = upper * bottom
        right_next = ends[k + 1, 2:3]
        coef[k, 0:1] = bottom
        coef[k, 1:2] = corner
        coef[k, 2:3] = head * bottom
        coef[k, 3:4] = ends[k, 1:2]
        coef[k, 4:5] = bottom * right_next
        coef[k, 5:6] = corner * right_next


def reduced_solve(first, last, coef, count):
    tops, lows = [], []
    for k in range(count - 1):
        shifted = last(k)
        if k:
            shifted = shifted + coef[k, 3:4] * tops[-1]
        follow = first(k + 1)
        tops.append(coef[k, 0:1] * shifted + coef[k, 1:2] * follow)
        lows.append(coef[k, 2:3] * shifted + coef[k, 0:1] * follow)
    for k in range(count - 3, -1, -1):
        tops[k] = tops[k] + coef[k, 5:6] * lows[k + 1]
        lows[k] = lows[k] + coef[k, 4:5] * lows[k + 1]
    zero = jnp.zeros_like(first(0))
    return lows + [zero], [zero] + tops


def kernel(
    nx,
    ny,
    ts_hbm,
    cs_hbm,
    tm_hbm,
    cm_hbm,
    al_hbm,
    ac_hbm,
    cf_hbm,
    bx_hbm,
    c2_hbm,
    by_hbm,
    ct_hbm,
    iz_hbm,
    out_t,
    out_c,
    cf,
    bxs,
    bx,
    c2,
    by,
    ct,
    iz,
    lu,
    lc,
    t_mid,
    c_mid,
    t_start,
    c_start,
    lu_second,
    lc_second,
    rate_t,
    rate_c,
    g,
    h,
    x_next,
    x_prev,
    mu,
    u,
    bycat,
    bxcat,
    izcat,
    diagonal,
    thick,
    cya,
    cyb,
    wy0,
    wy1,
    ly,
    ry,
    tm_coef,
    tc_coef,
    zr,
    zy,
    exs,
    exr,
    eys,
    eyr,
    coefx,
    coefy,
    xas,
    xar,
    xbs,
    xbr,
    yas,
    yar,
    ybs,
    ybr,
    eas,
    ear,
    eay,
    ebs,
    ebr,
    ebx,
    load_sem,
    store_sem,
    gx_send,
    gx_recv,
    gy_send,
    gy_recv,
):
    lx, lyn, nz = lu.shape
    rx = lyn // nx
    ryn = lx // ny
    mex = lax.axis_index("gx")
    mey = lax.axis_index("gy")
    sides = {"gx": (nx, mex, gx_send, gx_recv), "gy": (ny, mey, gy_send, gy_recv)}

    barrier = pltpu.get_barrier_semaphore()
    for axis, (count, me, _, _) in sides.items():
        for k in range(1, count):
            pl.semaphore_signal(
                barrier,
                inc=1,
                device_id={axis: lax.rem(me + k, count)},
                device_id_type=MESH,
            )

    quarter = lx // 4
    loads = [
        pltpu.make_async_copy(source, target, load_sem.at[n])
        for n, (source, target) in enumerate(
            (
                (cf_hbm, cf),
                (bx_hbm, bxs),
                (by_hbm, by),
                (bx_hbm, bx),
                (c2_hbm, c2),
                *(
                    (al_hbm.at[pl.ds(k * quarter, quarter)], lu.at[pl.ds(k * quarter, quarter)])
                    for k in range(4)
                ),
                (iz_hbm, iz),
                (ct_hbm, ct),
                (tm_hbm, t_mid),
                (cm_hbm, c_mid),
                (ac_hbm, lc),
                (ts_hbm, t_start),
                (cs_hbm, c_start),
            )
        )
    ]
    for load in loads:
        load.start()

    started = []

    def exchange(axis, kind, source, target):
        count, me, send, recv = sides[axis]
        copies = []
        for k in range(1, count):
            peer = lax.rem(me + k, count)
            copy = pltpu.make_async_remote_copy(
                src_ref=source(peer),
                dst_ref=target,
                send_sem=send.at[kind, k],
                recv_sem=recv.at[kind, k],
                device_id={axis: peer},
                device_id_type=MESH,
            )
            copy.start()
            copies.append(copy)
        started.extend(copies)
        return copies

    def arrive(copies):
        for copy in copies:
            copy.wait_recv()

    def row(value):
        return jnp.broadcast_to(value, (1, nz))

    wide = 4
    many = 8
    chunk = 32
    bf16 = jnp.bfloat16

    def stack(matrix, target):
        size = matrix.shape[0]
        part0 = matrix.astype(bf16)
        rest = matrix - part0.astype(jnp.float32)
        part1 = rest.astype(bf16)
        part2 = (rest - part1.astype(jnp.float32)).astype(bf16)
        for n, part in enumerate((part0, part1, part2)):
            target[n * size : (n + 1) * size] = jnp.concatenate([part, part], axis=1)

    def parted(value):
        high = value.astype(bf16)
        return high, (value - high.astype(jnp.float32)).astype(bf16)

    def stacked_dot(parts, value):
        size = value.shape[0]
        done = jnp.dot(
            parts[...],
            jnp.concatenate(parted(value), axis=0),
            preferred_element_type=jnp.float32,
        )
        return (done[2 * size :] + done[size : 2 * size]) + done[0:size]

    def thick_dot(value):
        count = value.shape[0]
        high, low = parted(value)
        rest = ((value - high.astype(jnp.float32)) - low.astype(jnp.float32)).astype(bf16)
        main = jnp.dot(
            jnp.concatenate([high, low, rest], axis=0), izcat[0], preferred_element_type=jnp.float32
        )
        fine = jnp.dot(
            jnp.concatenate([high, low], axis=0), izcat[1], preferred_element_type=jnp.float32
        )
        return (
            (main[2 * count :] + fine[count:]) + (main[count : 2 * count] + fine[0:count])
        ) + main[0:count]

    def prepare():
        face_low = explicit_part * ct[0:nz].reshape(1, nz)
        face_high = explicit_part * ct[1 : nz + 1].reshape(1, nz)
        lane = lax.broadcasted_iota(jnp.int32, (1, nz), 1)
        thick[0:1] = jnp.where(lane == 0, 0.0, face_low)
        thick[1:2] = jnp.where(lane == nz - 1, 0.0, face_high)
        def second_faces(j, carry):
            low, high = explicit_part * c2[j], explicit_part * c2[j + 1]
            cya[pl.ds(j, 1)] = row(low)
            cyb[pl.ds(j, 1)] = row(high)
            diagonal[pl.ds(j, 1)] = face_low + face_high + (low + high)
            return carry

        lax.fori_loop(0, lyn, second_faces, 0, unroll=8)
        ly[...] = wy0[...] * s0
        ry[...] = wy1[...] * s1

        matrix = iz[...]
        part0 = matrix.astype(bf16)
        izcat[0] = part0
        izcat[1] = (matrix - part0.astype(jnp.float32)).astype(bf16)

    for n in range(5):
        loads[n].wait()
    stack(by[...], bycat)
    stack(bx[...], bxcat)
    wy0[...] = jnp.broadcast_to(by[:, 0:1], (lyn, nz))
    wy1[...] = jnp.broadcast_to(by[:, lyn - 1 : lyn], (lyn, nz))
    eas[...] = jnp.zeros_like(eas)
    ebs[...] = jnp.zeros_like(ebs)
    zr[...] = jnp.zeros_like(zr)
    exs[...] = jnp.zeros_like(exs)
    eys[...] = jnp.zeros_like(eys)
    empty = jnp.zeros((lyn, nz), jnp.float32)

    def fold(value):
        return jnp.sum(value.reshape(-1, 8, nz), axis=0)

    def eliminate(i, keep):
        partial = 1.0 + cf[i] * keep
        scale = 1.0 / (partial + cf[i + 1])
        tm_coef[i] = scale
        tc_coef[i] = cf[i + 1] * scale
        return partial * scale

    lax.fori_loop(0, lx, eliminate, jnp.ones((1, nz), jnp.float32), unroll=4)
    def tips(i, carry):
        first, last = carry
        slab = lu[i]
        u[0, 0, i] = fold(slab * wy0[...])
        u[1, 0, i] = fold(slab * wy1[...])
        return first + bxs[i, 0] * slab, last + bxs[i, lx - 1] * slab

    first = last = empty
    for k in range(4):
        loads[5 + k].wait()
        first, last = lax.fori_loop(
            k * quarter, (k + 1) * quarter, tips, (first, last), unroll=4
        )

    for step in range(2):
        temper, cure = ((t_mid, c_mid), (t_start, c_start))[step]
        lu_now, lc_now = ((lu, lc), (lu_second, lc_second))[step]
        lu_then, lc_then = ((lu_second, lc_second), (lu, lc))[step]
        tip_x = stacked_dot(bycat, jnp.concatenate([first, last], axis=1))
        for d in range(nx):
            xas[step, d, 0] = tip_x[d * rx : (d + 1) * rx, 0:nz]
            xas[step, d, 1] = tip_x[d * rx : (d + 1) * rx, nz:]
        if step == 0:
            a0, a1 = cf[0], cf[lx]
            exs[0:1] = row(a0 * bxs[0, 0])
            exs[1:2] = row(a0 * bxs[0, lx - 1])
            exs[2:3] = row(a1 * bxs[lx - 1, 0])
            exs[3:4] = row(a1 * bxs[lx - 1, lx - 1])
            s0, s1 = c2[0], c2[lyn]
            eys[0:1] = row(by[0:1, 0:1]) * s0
            eys[1:2] = row(by[0:1, lyn - 1 : lyn]) * s0
            eys[2:3] = row(by[lyn - 1 : lyn, 0:1]) * s1
            eys[3:4] = row(by[lyn - 1 : lyn, lyn - 1 : lyn]) * s1
            pl.semaphore_wait(barrier, nx + ny - 2)
        out_xa = exchange("gx", 1 + 3 * step, lambda peer: xas.at[step, peer], xar.at[step, mex])
        eas[step, 0:1] = tip_x[0:1, 0:nz]
        eas[step, 1:2] = tip_x[0:1, nz:]
        eas[step, 2:3] = tip_x[lyn - 1 : lyn, 0:nz]
        eas[step, 3:4] = tip_x[lyn - 1 : lyn, nz:]
        out_ea = exchange("gy", 3 + 3 * step, lambda peer: eas.at[step], ear.at[step, mey])
        folded = [u[n, 0] if step == 0 else u[n, 0] + u[n, 1] for n in range(2)]
        tip_y = stacked_dot(bxcat, jnp.concatenate([jnp.sum(f, axis=1) for f in folded], axis=1))
        for d in range(ny):
            yas[step, d, 0] = tip_y[d * ryn : (d + 1) * ryn, 0:nz]
            yas[step, d, 1] = tip_y[d * ryn : (d + 1) * ryn, nz:]
        out_ya = exchange("gy", 1 + 3 * step, lambda peer: yas.at[step, peer], yar.at[step, mey])
        xar[step, mex] = xas[step, mex]
        yar[step, mey] = yas[step, mey]
        ear[step, mey] = eas[step]

        if step == 0:
            ends_x = exchange("gx", 0, lambda peer: exs, exr.at[mex])
            ends_y = exchange("gy", 0, lambda peer: eys, eyr.at[mey])
            exr[mex] = exs[...]
            eyr[mey] = eys[...]
            loads[9].wait()
            loads[10].wait()
            prepare()

        def through(n, carry):
            block = lu_now[pl.ds(n * many, many)].reshape(many * lyn, nz)
            high, low = parted(block)
            done = (
                jnp.dot(high, izcat[1], preferred_element_type=jnp.float32)
                + jnp.dot(low, izcat[0], preferred_element_type=jnp.float32)
                + jnp.dot(high, izcat[0], preferred_element_type=jnp.float32)
            )
            g[pl.ds(n * many, many)] = done.reshape(many, lyn, nz)
            return carry

        lax.fori_loop(0, lx // many, through, 0)

        def forward(n, before):
            solved = [stacked_dot(bycat, g[n * wide + k]) for k in range(wide)]
            for k in range(wide):
                i = n * wide + k
                before = (solved[k] + cf[i] * before) * tm_coef[i]
                h[i] = before
            return before

        if step == 1:
            lax.fori_loop(0, lx // wide, forward, empty)

        if step == 0:
            arrive(ends_x)
            arrive(ends_y)
            reduced_coefficients(exr, coefx, nx)
            reduced_coefficients(eyr, coefy, ny)
        arrive(out_xa)
        lows, tops = reduced_solve(
            lambda k: xar[step, k, 0], lambda k: xar[step, k, 1], coefx, nx
        )
        for d in range(nx):
            xbs[step, d, 0] = lows[d]
            xbs[step, d, 1] = tops[d]
        out_xb = exchange("gx", 2 + 3 * step, lambda peer: xbs.at[step, peer], xbr.at[step, mex])
        arrive(out_ea)
        lows, tops = reduced_solve(
            lambda k: ear[step, k, 0:2], lambda k: ear[step, k, 2:4], coefy, ny
        )
        for d in range(ny):
            eay[d, 0:2] = lows[d]
            eay[d, 2:4] = tops[d]
        edge = eay[mey]
        ebs[step, 0:1] = edge[0:1]
        ebs[step, 1:2] = edge[2:3]
        ebs[step, 2:3] = edge[1:2]
        ebs[step, 3:4] = edge[3:4]
        out_eb = exchange("gx", 3 + 3 * step, lambda peer: ebs.at[step], ebr.at[step, mex])
        arrive(out_ya)
        lows, tops = reduced_solve(
            lambda k: yar[step, k, 0], lambda k: yar[step, k, 1], coefy, ny
        )
        for d in range(ny):
            ybs[step, d, 0] = lows[d]
            ybs[step, d, 1] = tops[d]
        out_yb = exchange("gy", 2 + 3 * step, lambda peer: ybs.at[step, peer], ybr.at[step, mey])
        xbr[step, mex] = xbs[step, mex]
        ybr[step, mey] = ybs[step, mey]
        ebr[step, mex] = ebs[step]

        inside = slice(MARGIN, MARGIN + lyn)

        if step == 0:
            lax.fori_loop(0, lx // wide, forward, empty)

        def backward(n, after):
            i = lx - 1 - n
            value = h[i] + tc_coef[i] * after
            g[i] = value
            return value

        lax.fori_loop(0, lx, backward, empty, unroll=4)

        if step == 0:
            for n in (11, 12, 13):
                loads[n].wait()
        else:
            loads[14].wait()
            loads[15].wait()

        def rates(i, carry):
            heating = jnp.exp(arrhenius * temper[i])
            value = cure[i]
            remain = 1.0 - value
            grown = initial_rate + value
            rate_t[i] = (heat_release * arrhenius) * (heating * grown * remain * remain)
            rate_c[i] = (heat_release * heating) * (remain * remain - 2.0 * grown * remain)
            return carry

        lax.fori_loop(0, lx, rates, 0, unroll=2)

        arrive(out_yb)
        for d in range(ny):
            zy[d * ryn : (d + 1) * ryn] = ybr[step, d, 0]
            zy[lx + d * ryn : lx + (d + 1) * ryn] = ybr[step, d, 1]
        zy[...] = thick_dot(zy[...])

        def beside(i, carry):
            h[i] = g[i] + ly[...] * zy[pl.ds(lx + i, 1)] + ry[...] * zy[pl.ds(i, 1)]
            return carry

        lax.fori_loop(0, lx, beside, 0, unroll=4)

        arrive(out_eb)
        lows, tops = reduced_solve(
            lambda k: ebr[step, k, 0:2], lambda k: ebr[step, k, 2:4], coefx, nx
        )
        for d in range(nx):
            ebx[d, 0:2] = lows[d]
            ebx[d, 2:4] = tops[d]
        arrive(out_xb)
        for d in range(nx):
            zr[d * rx : (d + 1) * rx] = xbr[step, d, 0]
            zr[lyn + d * rx : lyn + (d + 1) * rx] = xbr[step, d, 1]
        corner = 2 * lyn
        zr[corner : corner + 4] = ebx[mex, 0:4]
        zr[...] = thick_dot(zr[...])
        next_next = zr[corner : corner + 1]
        next_prev = zr[corner + 1 : corner + 2]
        prev_next = zr[corner + 2 : corner + 3]
        prev_prev = zr[corner + 3 : corner + 4]
        value = zr[0:lyn] + ly[...] * next_prev + ry[...] * next_next
        x_next[...] = value
        mu[lx + 1, inside] = value
        value = zr[lyn : 2 * lyn] + ly[...] * prev_prev + ry[...] * prev_next
        x_prev[...] = value
        mu[0, inside] = value

        def correct(i, carry):
            left = a0 * bxs[0, i]
            right = a1 * bxs[lx - 1, i]
            y_next = zy[pl.ds(i, 1)]
            y_prev = zy[pl.ds(lx + i, 1)]
            mu[i + 1, inside] = h[i] + left * x_prev[...] + right * x_next[...]
            mu[i + 1, MARGIN - 1 : MARGIN] = y_prev + left * prev_prev + right * next_prev
            mu[i + 1, MARGIN + lyn : MARGIN + lyn + 1] = (
                y_next + left * prev_next + right * next_next
            )
            return carry

        lax.fori_loop(0, lx, correct, 0, unroll=4)

        stores = []
        firsts, lasts = [], []
        group = 4
        for part, y in enumerate(range(0, lyn, chunk)):
            here = slice(y, y + chunk)
            start = MARGIN + y

            def update(n, carry):
                first, last = carry
                i = n * group
                flux = (explicit_part * cf[i]) * (
                    mu[i + 1, start : start + chunk] - mu[i, start : start + chunk]
                )
                for k in range(group):
                    i = n * group + k
                    value = mu[i + 1, start : start + chunk]
                    follow = (explicit_part * cf[i + 1]) * (
                        mu[i + 2, start : start + chunk] - value
                    )
                    kick = (
                        (flux - follow)
                        + diagonal[here] * value
                        - cya[here] * mu[i + 1, start - 1 : start + chunk - 1]
                        - cyb[here] * mu[i + 1, start + 1 : start + chunk + 1]
                        - thick[0:1] * pltpu.roll(value, 1, 1)
                        - thick[1:2] * pltpu.roll(value, nz - 1, 1)
                    )
                    flux = follow
                    old = lc_now[i, here]
                    source = value + (cure_step / heat_release) * old
                    new = lu_now[i, here] - kick + rate_t[i, here] * source
                    lu_then[i, here] = new
                    lc_then[i, here] = old + rate_c[i, here] * source
                    if step == 0:
                        first = first + bxs[i, 0] * new
                        last = last + bxs[i, lx - 1] * new
                        u[0, part, i] = fold(new * wy0[here])
                        u[1, part, i] = fold(new * wy1[here])
                return first, last

            none = jnp.zeros((chunk, nz), jnp.float32)
            first = last = none
            steps = lx // group // 2
            for half in range(2):
                first, last = lax.fori_loop(
                    half * steps, (half + 1) * steps, update, (first, last)
                )
                if step == 1:
                    rows = pl.ds(half * steps * group, steps * group)
                    for n, (source, target) in enumerate(((lu, out_t), (lc, out_c))):
                        store = pltpu.make_async_copy(
                            source.at[rows, pl.ds(y, chunk)],
                            target.at[rows, pl.ds(y, chunk)],
                            store_sem.at[n, part, half],
                        )
                        store.start()
                        stores.append(store)
            firsts.append(first)
            lasts.append(last)
        first = jnp.concatenate(firsts, axis=0)
        last = jnp.concatenate(lasts, axis=0)
        for store in stores:
            store.wait()
    for copy in started:
        copy.wait_send()


def hand_out(first, second, out_first, out_second, held, sem):
    chunks = held.shape[1]
    size = first.shape[0] // chunks
    arrivals, departures = [], []
    for part in range(chunks):
        rows = pl.ds(part * size, size)
        for n, (source, target) in enumerate(((first, out_first), (second, out_second))):
            slot = held.at[n, part]
            arrivals.append(pltpu.make_async_copy(source.at[rows], slot, sem.at[0, n, part]))
            departures.append(pltpu.make_async_copy(slot, target.at[rows], sem.at[1, n, part]))
    for copy in arrivals:
        copy.start()
    for arrival, departure in zip(arrivals, departures):
        arrival.wait()
        departure.start()
    for copy in departures:
        copy.wait()


def per_device(nx, ny, ts, cs, tm, cm, al, ac, cf, bx, c2, by, ct, iz):
    lx, lyn, nz = al.shape
    f32 = jnp.float32
    vm = pltpu.VMEM
    tile = (lx, lyn, nz)
    anywhere = pl.BlockSpec(memory_space=pl.ANY)
    hbm = pl.BlockSpec(memory_space=pltpu.HBM)
    sm = pltpu.SMEM
    rx, ryn = lyn // nx, lx // ny
    scratch = (
        [sm(cf.shape, f32), sm(bx.shape, f32), vm(bx.shape, f32), sm(c2.shape, f32)]
        + [vm(by.shape, f32), vm((nz + 1,), f32), vm(iz.shape, f32)]
        + [vm(tile, f32)] * 12
        + [vm((lyn, nz), f32)] * 2
        + [vm((lx + 2, lyn + 2 * MARGIN, nz), f32), vm((2, 2, lx, 8, nz), f32)]
        + [vm((3 * lyn, 2 * lyn), jnp.bfloat16), vm((3 * lx, 2 * lx), jnp.bfloat16)]
        + [vm((2, nz, nz), jnp.bfloat16), vm((lyn, nz), f32), vm((8, nz), f32)]
        + [vm((lyn, nz), f32)] * 6
        + [vm((lx, 1, nz), f32)] * 2
        + [vm((2 * lyn + 16, nz), f32), vm((2 * lx, nz), f32)]
        + [vm((8, nz), f32), vm((nx, 8, nz), f32), vm((8, nz), f32), vm((ny, 8, nz), f32)]
        + [vm((nx, 8, nz), f32), vm((ny, 8, nz), f32)]
        + [vm((2, nx, 2, rx, nz), f32)] * 4
        + [vm((2, ny, 2, ryn, nz), f32)] * 4
        + [vm((2, 8, nz), f32), vm((2, ny, 8, nz), f32), vm((ny, 8, nz), f32)]
        + [vm((2, 8, nz), f32), vm((2, nx, 8, nz), f32), vm((nx, 8, nz), f32)]
        + [pltpu.SemaphoreType.DMA((16,)), pltpu.SemaphoreType.DMA((2, lyn // 32, 2))]
        + [pltpu.SemaphoreType.DMA((7, nx))] * 2
        + [pltpu.SemaphoreType.DMA((7, ny))] * 2
    )
    results = pl.pallas_call(
        functools.partial(kernel, nx, ny),
        out_shape=(jax.ShapeDtypeStruct(tile, f32), jax.ShapeDtypeStruct(tile, f32)),
        in_specs=[hbm] * 12,
        out_specs=(anywhere, anywhere),
        scratch_shapes=scratch,
        compiler_params=pltpu.CompilerParams(
            collective_id=0, has_side_effects=True, vmem_limit_bytes=60 * 1024 * 1024
        ),
    )(ts, cs, tm, cm, al, ac, cf, bx, c2, by, ct, iz)
    return pl.pallas_call(
        hand_out,
        out_shape=(jax.ShapeDtypeStruct(tile, f32), jax.ShapeDtypeStruct(tile, f32)),
        in_specs=[anywhere] * 2,
        out_specs=(hbm, hbm),
        scratch_shapes=[vm((2, 8, lx // 8, lyn, nz), f32), pltpu.SemaphoreType.DMA((2, 2, 8))],
        compiler_params=pltpu.CompilerParams(vmem_limit_bytes=60 * 1024 * 1024),
    )(*results)


def solution(mesh):
    tile = P("gx", "gy", None)
    placed = (tile,) * 6 + (P("gx"), P("gx", None), P("gy"), P("gy", None), P(), P())
    return jax.shard_map(
        functools.partial(per_device, mesh.shape["gx"], mesh.shape["gy"]),
        mesh=mesh,
        in_specs=placed,
        out_specs=(tile, tile),
        check_vma=False,
    )
```
